32 devices in a mesh: run: 1, row: 16 (over z, y, core), col: 1, seg: 2 (over x).
Axes of the slice: x: 2, y: 2, z: 4, core: 2. Of those that a mesh axis runs over, the one named last changes fastest.
Arguments:
- traces: bfloat16 [2, 1024, 2048], P(('run', 'seg'), 'row', 'col'), may hold values from -30 to 30
- live_mask: int32 [1024], P(('run', 'row')), may hold values 0 or 1
- sources: int32 [64], replicated, may hold values from 0 to 1023
- owners: int32 [64, 1], replicated, may hold values from 0 to 15; in each aligned block of 64 rows (0 to 63, 64 to 127, ...) at most 12 rows name the same one
Outputs:
- gathers: bfloat16 [192, 16, 64, 256], P(('run', 'row'), None, ('col', 'seg'))
The draws below stay inside these ranges and needn't reach their ends.
Inputs may be any that keep to these rules, and one draw needn't show every extreme that they name: `owners`: at most 12 sources share an owner, and some owner has exactly 12.
All inputs are finite; a program needn't handle non-finite values. No bound on the sum of `live_mask` on one device may be relied on, other than what follows from the above.
Results may differ from the reference program's by a relative error of at most 0.024.
Values may be sent and summed in bfloat16 or wider, within the bound.
A program may use at most 64 MiB of HBM per device.

```python
import math
import jax
import jax.numpy as jnp
import numpy as np
from jax import lax

NT = 2048
NF = 1024
LAGS = 256
BAND = 64
CB = 64
V = 64
NSEG = 2
CH = 1024
CAP = 12
N_ROW = 16
N_COL = 1


def draw_traces(key, part):
    keys = jax.random.split(jax.random.fold_in(key, 7), 5)
    shape = (NSEG, CH, NT)
    noise = jnp.clip(jax.random.normal(keys[0], shape, jnp.float32), -5.0, 5.0)
    amplitude = jnp.exp(jax.random.uniform(keys[1], (NSEG, CH, 1), jnp.float32, math.log(0.3), math.log(3.0)))
    tone_bins = jax.random.randint(keys[2], (1, CH, 1), 1, NF)
    tone_size = jnp.exp(jax.random.uniform(keys[3], (1, CH, 1), jnp.float32, math.log(0.2), math.log(1.0)))
    tone_phase = jax.random.uniform(keys[4], (1, CH, 1), jnp.float32, -math.pi, math.pi)
    sample_ids = jnp.arange(NT, dtype=jnp.int32)[None, None, :]
    angles = (tone_bins * sample_ids % NT).astype(jnp.float32) * (2.0 * math.pi / NT) + tone_phase
    return (amplitude * (noise + tone_size * jnp.cos(angles))).astype(jnp.bfloat16)


def place_ends(drawn, stream_key, smallest, high):
    index_at = [jax.random.randint(jax.random.fold_in(stream_key, axis), (), 0, length) for axis, length in enumerate(drawn.shape)]
    widest = drawn.shape.index(max(drawn.shape))
    beside = index_at[:widest] + [(index_at[widest] + 1) % drawn.shape[widest]] + index_at[widest + 1:]
    return drawn.at[tuple(index_at)].set(smallest).at[tuple(beside)].set(high)


def deal_out(key, own, number, rows, number_of, top, reach, lean):
    order = jax.random.permutation(key, number_of)
    crowded, ordinary = shares(number_of, rows * top, reach, lean, True), shares(number_of, rows * top, reach, lean, False)
    places = jnp.arange(number_of)

    def named(sizes, offset_by):
        used = int((sizes > 0).sum())
        fixed = max(1, used // 4)
        moved = fixed + (places - fixed + offset_by * (used - fixed)) % max(1, number_of - fixed)
        return jnp.zeros((number_of,), jnp.int32).at[order[jnp.where(places < fixed, places, moved)]].set(jnp.asarray(sizes, jnp.int32))

    sizes = jnp.where(number % 4 == 0, named(crowded, number // 4), named(ordinary, number - number // 4 - 1))
    mixed = jax.random.permutation(jax.random.fold_in(own, 3), number_of)
    source_of, sink = mixed[0:number_of // 2 * 2:2], mixed[1:number_of // 2 * 2:2]
    room = jnp.minimum(sizes[source_of] - 1, reach - sizes[sink]) // 2
    room = jnp.where((source_of == order[0]) | (sink == order[0]) | (sizes[sink] == 0), 0, jnp.maximum(room, 0))
    moved = jax.random.randint(jax.random.fold_in(own, 4), (number_of // 2,), 0, 1 << 20) % (room + 1)
    sizes = sizes.at[source_of].add(-moved).at[sink].add(moved)
    labels = jnp.searchsorted(jnp.cumsum(sizes), jnp.arange(rows * top), side="right").astype(jnp.int32)
    table = labels.reshape(top, rows).T
    table = table[jax.random.permutation(jax.random.fold_in(own, 1), rows)]
    offset_by = jax.random.randint(jax.random.fold_in(own, 2), (rows, 1), 0, top)
    return jnp.take_along_axis(table, (jnp.arange(top)[None, :] + offset_by) % top, axis=1)


def shares(amount, total, bound, skew, full):
    weights = [(1 << 20) // math.isqrt(standing ** skew) + 1 for standing in range(1, amount + 1)]
    largest = bound if full else min(bound, max(-(-total // amount), total * weights[0] // sum(weights)))
    least = 1 if total - largest >= amount - 1 else 0
    given, surplus = [largest] + [least] * (amount - 1), total - largest - least * (amount - 1)
    while surplus > 0:
        movable = [i for i in range(1, amount) if given[i] < largest] or [i for i in range(1, amount) if given[i] < bound]
        mass, remaining = sum([weights[i] for i in movable]), surplus
        for i in movable:
            extra = min(bound - given[i], max(1, remaining * weights[i] // mass), surplus)
            given[i] = given[i] + extra
            surplus = surplus - extra
    return np.array(given)


def setup_inputs(seed: int = 0, part: int = 0) -> dict:
    arg_keys = jax.random.split(jax.random.key(seed), 5)
    part_splits = jax.random.split(jax.random.fold_in(arg_keys[4], part), 5)
    traces = draw_traces(jax.random.fold_in(jax.random.fold_in(arg_keys[4], part), 71), part)
    live_mask = place_ends((jax.random.randint(part_splits[1], (CH,), 0, 16) < 15).astype(jnp.int32), jax.random.fold_in(part_splits[1], 1), 0, 1)
    sources = place_ends(jax.random.randint(arg_keys[2], (V,), 0, CH), jax.random.fold_in(arg_keys[2], 1), 0, CH - 1).astype(jnp.int32)
    owners_keys = jax.random.split(jax.random.fold_in(arg_keys[3], 1), V // V)
    owners_turns = jax.random.permutation(jax.random.fold_in(arg_keys[3], 3), V // V)
    owners = jax.vmap(lambda own, number: deal_out(jax.random.fold_in(arg_keys[3], 2), own, number, V, N_ROW, 1, CAP, 2))(owners_keys, owners_turns).reshape((V, 1))
    return {"traces": traces, "live_mask": live_mask, "sources": sources, "owners": owners}


two_pi = 2.0 * math.pi

def turn_table(first_ids, second_ids, period):
    product = first_ids[:, None] * second_ids[None, :] % period
    return product.astype(jnp.float32) * (two_pi / period)

def reference(traces, live_mask, sources, owners):
    sample_ids = jnp.arange(NT, dtype=jnp.int32)
    bin_ids = jnp.arange(NF, dtype=jnp.int32)
    angles = turn_table(sample_ids, bin_ids, NT)
    cosine = jnp.cos(angles).astype(jnp.bfloat16)
    sine_table = jnp.sin(angles).astype(jnp.bfloat16)
    flat = traces.reshape(NSEG * CH, NT)
    real_part = jnp.dot(flat, cosine, preferred_element_type=jnp.float32)
    imag_part = -jnp.dot(flat, sine_table, preferred_element_type=jnp.float32)
    band_power = (real_part * real_part + imag_part * imag_part).reshape(NSEG * CH, NF // BAND, BAND)
    band_power = lax.optimization_barrier(jnp.sum(band_power, axis=-1)) / (2 * BAND) + 1e-05
    living = jnp.tile(live_mask.astype(jnp.float32), NSEG)
    scaling = living[:, None] / jnp.sqrt(band_power)
    scaling = jnp.repeat(scaling, BAND, axis=1)
    white_real = (real_part * scaling).astype(jnp.bfloat16).reshape(NSEG, CH, NF)
    white_imag = (imag_part * scaling).astype(jnp.bfloat16).reshape(NSEG, CH, NF)
    source_real = white_real[:, sources, :]
    source_imag = white_imag[:, sources, :]
    lag_ids = jnp.arange(LAGS, dtype=jnp.int32) - LAGS // 2 + NT
    lag_angles = turn_table(bin_ids, lag_ids, NT)
    lag_cos = jnp.cos(lag_angles).astype(jnp.bfloat16)
    lag_sin = jnp.sin(lag_angles).astype(jnp.bfloat16)
    half_bins = NF // N_COL
    block_rows = min(CH, 128)

    def receiver_block(first_row):
        total = jnp.zeros((block_rows, V, LAGS), jnp.float32)
        for segment in range(NSEG):
            for half in range(N_COL):
                low = half * half_bins
                high = low + half_bins
                recv_real = lax.dynamic_slice_in_dim(white_real[segment, :, low:high], first_row, block_rows, 0).astype(jnp.float32)
                recv_imag = lax.dynamic_slice_in_dim(white_imag[segment, :, low:high], first_row, block_rows, 0).astype(jnp.float32)
                real_source = source_real[segment, :, low:high].astype(jnp.float32)
                imag_source = source_imag[segment, :, low:high].astype(jnp.float32)
                cross_real = (real_source[None, :, :] * recv_real[:, None, :] + imag_source[None, :, :] * recv_imag[:, None, :]).astype(jnp.bfloat16)
                cross_imag = (imag_source[None, :, :] * recv_real[:, None, :] - real_source[None, :, :] * recv_imag[:, None, :]).astype(jnp.bfloat16)
                table = jnp.concatenate([lag_cos[low:high], -lag_sin[low:high]], axis=0).astype(jnp.float32)
                stacked_cross = jnp.concatenate([cross_real, cross_imag], axis=2).astype(jnp.float32)
                term = jnp.einsum('gvf,fl->gvl', stacked_cross, table)
                total = total + lax.optimization_barrier(term.astype(jnp.bfloat16)).astype(jnp.float32)
        return total
    starts = jnp.arange(CH // block_rows, dtype=jnp.int32) * block_rows
    stacked = lax.map(receiver_block, starts).reshape(CH, V, LAGS)
    mean_sq = lax.optimization_barrier(jnp.mean(stacked * stacked, axis=-1, keepdims=True))
    normed = (stacked / jnp.sqrt(mean_sq + 1e-06)).astype(jnp.bfloat16)
    owner_ids = owners[:, 0]
    order_ids = jnp.arange(V, dtype=jnp.int32)
    earlier = (owner_ids[:, None] == owner_ids[None, :]) & (order_ids[None, :] < order_ids[:, None])
    slot_rank = lax.optimization_barrier(jnp.sum(earlier.astype(jnp.int32), axis=1))
    slot_ids = (owner_ids * CAP + slot_rank).astype(jnp.int32)
    gathers = jnp.zeros((N_ROW * CAP, CH, LAGS), jnp.bfloat16).at[slot_ids].set(jnp.transpose(normed, (1, 0, 2)))
    return gathers.reshape(N_ROW * CAP, N_ROW, CB, LAGS)
```

```python
import math
from functools import partial

import jax
import jax.numpy as jnp
import numpy as np
from jax import lax
from jax.experimental import pallas as pl
from jax.experimental.pallas import tpu as pltpu
from jax.sharding import PartitionSpec as P

NT = 2048
NF = 1024
LAGS = 256
BAND = 64


two_pi = 2.0 * math.pi


def turn_table(first_ids, second_ids, period):
    product = first_ids[:, None] * second_ids[None, :] % period
    return product.astype(jnp.float32) * (two_pi / period)


def lag_matrix(bin_ids):
    lag_ids = jnp.arange(LAGS, dtype=jnp.int32) - LAGS // 2 + NT
    lag_angles = turn_table(bin_ids, lag_ids, NT)
    return jnp.concatenate(
        [jnp.cos(lag_angles).astype(jnp.bfloat16), -jnp.sin(lag_angles).astype(jnp.bfloat16)],
        axis=0,
    )


def correlate(recv_real, recv_imag, real_source, imag_source, lag_table):
    cross_real = (
        real_source[:, None, :] * recv_real[:, :, None]
        + imag_source[:, None, :] * recv_imag[:, :, None]
    ).astype(jnp.bfloat16)
    cross_imag = (
        imag_source[:, None, :] * recv_real[:, :, None]
        - real_source[:, None, :] * recv_imag[:, :, None]
    ).astype(jnp.bfloat16)
    stacked_cross = jnp.concatenate([cross_real, cross_imag], axis=0)
    return jnp.einsum("fl,fgv->gvl", lag_table, stacked_cross, preferred_element_type=jnp.float32)


def local(traces, live_mask, sources, owners):
    col_count = lax.axis_size("col")
    seg_count = lax.axis_size("seg")
    row_count = lax.axis_size("row")
    samples = traces[0]
    channels = samples.shape[0]
    local_width = samples.shape[1]
    num_sources = sources.shape[0]
    first_sample = lax.axis_index("col") * local_width
    half_bins = NF // col_count
    sample_ids = first_sample + jnp.arange(local_width, dtype=jnp.int32)
    bin_ids = jnp.arange(half_bins * lax.axis_size("col"), dtype=jnp.int32)
    angles = turn_table(sample_ids, bin_ids, NT)
    cosine = jnp.cos(angles).astype(jnp.bfloat16)
    sine_table = jnp.sin(angles).astype(jnp.bfloat16)
    real_part = jnp.einsum("tf,ct->fc", cosine, samples, preferred_element_type=jnp.float32)
    imag_part = -jnp.einsum("tf,ct->fc", sine_table, samples, preferred_element_type=jnp.float32)
    spectra = lax.psum_scatter(
        jnp.concatenate([real_part, imag_part], axis=1).astype(jnp.bfloat16),
        "col",
        scatter_dimension=0,
        tiled=True,
    ).astype(jnp.float32)
    squares = (spectra * spectra).reshape(half_bins // BAND, BAND, 2, channels)
    band_power = jnp.sum(squares, axis=(1, 2)) / (2 * BAND) + 1e-05
    scaling = live_mask.astype(jnp.float32)[None, :] / jnp.sqrt(band_power)
    scaling = jnp.repeat(scaling, BAND, axis=0)
    whitened = (
        (spectra.reshape(half_bins, 2, channels) * scaling[:, None, :])
        .reshape(half_bins, 2 * channels)
        .astype(jnp.bfloat16)
    )
    white_real = whitened[:, :channels]
    white_imag = whitened[:, channels:]
    everyone = lax.all_gather(whitened, "row", axis=1, tiled=True)
    block_ids = sources // channels
    within = sources % channels
    real_cols = block_ids * (2 * channels) + within
    source_real = jnp.take(everyone, real_cols, axis=1)
    source_imag = jnp.take(everyone, real_cols + channels, axis=1)
    receivers = channels // (col_count * seg_count)
    bin_ids = lax.axis_index("col") * half_bins + jnp.arange(half_bins, dtype=jnp.int32)
    lag_table = lag_matrix(bin_ids)
    real_source = source_real.astype(jnp.float32)
    imag_source = source_imag.astype(jnp.float32)

    def one_group(offset):
        recv_real = lax.dynamic_slice_in_dim(white_real, offset, receivers, 1).astype(jnp.float32)
        recv_imag = lax.dynamic_slice_in_dim(white_imag, offset, receivers, 1).astype(jnp.float32)
        return correlate(recv_real, recv_imag, real_source, imag_source, lag_table)

    offsets = (
        jnp.arange(receivers * lax.axis_size(("col", "seg")) // receivers, dtype=jnp.int32)
        * receivers
    )
    blocks = lax.map(one_group, offsets)
    stacked = lax.psum_scatter(
        blocks.reshape(receivers * lax.axis_size(("col", "seg")), num_sources, LAGS).astype(
            jnp.bfloat16
        ),
        ("col", "seg"),
        scatter_dimension=0,
        tiled=True,
    ).astype(jnp.float32)
    mean_sq = jnp.mean(stacked * stacked, axis=-1, keepdims=True)
    normed = (stacked / jnp.sqrt(mean_sq + 1e-06)).astype(jnp.bfloat16)
    capacity = 3 * num_sources // row_count
    owner_ids = owners[:, 0]
    order_ids = jnp.arange(num_sources, dtype=jnp.int32)
    earlier = (owner_ids[:, None] == owner_ids[None, :]) & (order_ids[None, :] < order_ids[:, None])
    slot_rank = jnp.sum(earlier.astype(jnp.int32), axis=1)
    slot_ids = owner_ids * capacity + slot_rank
    placing = (
        jnp.arange(row_count * capacity, dtype=jnp.int32)[:, None] == slot_ids[None, :]
    ).astype(jnp.bfloat16)
    outgoing = jnp.einsum(
        "sv,gvl->sgl", placing, normed, preferred_element_type=jnp.float32
    ).astype(jnp.bfloat16)
    return lax.all_to_all(outgoing[:, None], "row", split_axis=0, concat_axis=1, tiled=True)


def host_tables(num_samples):
    samples = np.arange(num_samples, dtype=np.int64)
    bins = np.arange(NF, dtype=np.int64)
    angles = (samples[:, None] * bins[None, :] % NT) * (two_pi / NT)
    forward = np.concatenate([np.cos(angles), -np.sin(angles)], axis=1)
    lags = np.arange(LAGS, dtype=np.int64) - LAGS // 2 + NT
    lag_angles = (bins[:, None] * lags[None, :] % NT) * (two_pi / NT)
    back = np.concatenate([np.cos(lag_angles), -np.sin(lag_angles)], axis=0)
    return forward.astype(jnp.bfloat16), back.astype(jnp.bfloat16)


def whitened_spectra(samples, forward):
    rows = samples.shape[0]
    spectra = jnp.dot(samples, forward, preferred_element_type=jnp.float32)
    power = jnp.sum((spectra * spectra).reshape(rows, 2, NF // BAND, BAND), axis=(1, 3))
    scaling = 1.0 / jnp.sqrt(power / (2 * BAND) + 1e-05)
    scaling = jnp.repeat(scaling, BAND, axis=1)
    return (spectra * jnp.concatenate([scaling, scaling], axis=1)).astype(jnp.bfloat16)


def gather_kernel(recv_ref, source_ref, back_ref, out_ref, cross_ref):
    segments, slots, _ = source_ref.shape
    receivers = recv_ref.shape[2]
    for slot in range(slots):
        real = imag = None
        for seg in range(segments):
            recv_real = recv_ref[0, seg, :, :NF]
            recv_imag = recv_ref[0, seg, :, NF:]
            source_real = source_ref[seg, slot : slot + 1, :NF]
            source_imag = source_ref[seg, slot : slot + 1, NF:]
            term_real = source_real * recv_real + source_imag * recv_imag
            term_imag = source_imag * recv_real - source_real * recv_imag
            real = term_real if real is None else real + term_real
            imag = term_imag if imag is None else imag + term_imag
        rows = pl.ds(slot * receivers, receivers)
        cross_ref[rows, :NF] = real
        cross_ref[rows, NF:] = imag
    stacked = jnp.dot(cross_ref[...], back_ref[...], preferred_element_type=jnp.float32)
    mean_sq = jnp.mean(stacked * stacked, axis=-1, keepdims=True)
    normed = stacked * lax.rsqrt(mean_sq + 1e-06)
    out_ref[...] = normed.astype(out_ref.dtype).reshape(out_ref.shape)


def correlate_gathers(everyone, sources, back):
    blocks, segments, receivers, width = everyone.shape
    slots = sources.shape[1]
    return pl.pallas_call(
        gather_kernel,
        grid=(blocks,),
        in_specs=[
            pl.BlockSpec((1, segments, receivers, width), lambda b: (b, 0, 0, 0)),
            pl.BlockSpec((segments, slots, width), lambda b: (0, 0, 0)),
            pl.BlockSpec((width, LAGS), lambda b: (0, 0)),
        ],
        out_specs=pl.BlockSpec((slots, 1, receivers, LAGS), lambda b: (0, b, 0, 0)),
        out_shape=jax.ShapeDtypeStruct((slots, blocks, receivers, LAGS), jnp.bfloat16),
        scratch_shapes=[pltpu.VMEM((slots * receivers, width), jnp.bfloat16)],
        compiler_params=pltpu.CompilerParams(vmem_limit_bytes=40 << 20),
        cost_estimate=pl.CostEstimate(
            flops=2 * slots * blocks * receivers * width * LAGS,
            bytes_accessed=2 * blocks * receivers * (segments * width + slots * LAGS),
            transcendentals=0,
        ),
    )(everyone, sources, back)


def slot_channels(sources, owners, row_count):
    num_sources = sources.shape[0]
    capacity = 3 * num_sources // row_count
    owner_ids = owners[:, 0]
    order_ids = jnp.arange(num_sources, dtype=jnp.int32)
    earlier = (owner_ids[:, None] == owner_ids[None, :]) & (order_ids[None, :] < order_ids[:, None])
    slot_ids = owner_ids * capacity + jnp.sum(earlier.astype(jnp.int32), axis=1)
    placing = jnp.arange(row_count * capacity, dtype=jnp.int32)[:, None] == slot_ids[None, :]
    return jnp.sum(jnp.where(placing, sources[None, :] + 1, 0), axis=1) - 1


def paired(forward, back, traces, live_mask, sources, owners):
    row_count = lax.axis_size("row")
    seg = lax.axis_index("seg")
    channels, width = traces.shape[1:]
    receivers = channels // 2
    samples = traces[0] * live_mask.astype(traces.dtype)[:, None]
    channel_of = slot_channels(sources, owners, row_count)
    first = lax.axis_index("row") * channels
    picking = channel_of[:, None] == first + jnp.arange(channels, dtype=jnp.int32)[None, :]
    picked = jnp.dot(
        picking.astype(traces.dtype), samples, preferred_element_type=jnp.float32
    ).astype(traces.dtype)
    swap = [(0, 1), (1, 0)]
    kept = lax.dynamic_slice_in_dim(samples, seg * receivers, receivers, 0)
    given = lax.dynamic_slice_in_dim(samples, (1 - seg) * receivers, receivers, 0)
    taken = lax.ppermute(given, "seg", swap)
    white = whitened_spectra(jnp.concatenate([kept, taken], axis=0), forward)
    everyone = lax.all_gather(white.reshape(2, receivers, 2 * NF), "row", axis=0)
    mine = lax.psum_scatter(picked, "row", scatter_dimension=0, tiled=True)
    slots = mine.shape[0]
    other = lax.ppermute(mine, "seg", swap)
    white_sources = whitened_spectra(jnp.concatenate([mine, other], axis=0), forward)
    return correlate_gathers(everyone, white_sources.reshape(2, slots, 2 * NF), back)


def solution(mesh):
    placed = (P(("run", "seg"), "row", "col"), P(("run", "row")), P(), P())
    body = local
    if mesh.shape["col"] == 1 and mesh.shape["seg"] == 2:
        forward, back = host_tables(NT)
        body = partial(paired, forward, back)
    return jax.shard_map(
        body,
        mesh=mesh,
        in_specs=placed,
        out_specs=P(("run", "row"), None, ("col", "seg"), None),
        check_vma=False,
    )
```

```python
import math
from functools import partial

import jax
import jax.numpy as jnp
import numpy as np
from jax import lax
from jax.experimental import pallas as pl
from jax.experimental.pallas import tpu as pltpu
from jax.sharding import PartitionSpec as P

NT = 2048
NF = 1024
LAGS = 256
BAND = 64


two_pi = 2.0 * math.pi


def turn_table(first_ids, second_ids, period):
    product = first_ids[:, None] * second_ids[None, :] % period
    return product.astype(jnp.float32) * (two_pi / period)


def lag_matrix(bin_ids):
    lag_ids = jnp.arange(LAGS, dtype=jnp.int32) - LAGS // 2 + NT
    lag_angles = turn_table(bin_ids, lag_ids, NT)
    return jnp.concatenate(
        [jnp.cos(lag_angles).astype(jnp.bfloat16), -jnp.sin(lag_angles).astype(jnp.bfloat16)],
        axis=0,
    )


def correlate(recv_real, recv_imag, real_source, imag_source, lag_table):
    cross_real = (
        real_source[:, None, :] * recv_real[:, :, None]
        + imag_source[:, None, :] * recv_imag[:, :, None]
    ).astype(jnp.bfloat16)
    cross_imag = (
        imag_source[:, None, :] * recv_real[:, :, None]
        - real_source[:, None, :] * recv_imag[:, :, None]
    ).astype(jnp.bfloat16)
    stacked_cross = jnp.concatenate([cross_real, cross_imag], axis=0)
    return jnp.einsum("fl,fgv->gvl", lag_table, stacked_cross, preferred_element_type=jnp.float32)


def local(traces, live_mask, sources, owners):
    col_count = lax.axis_size("col")
    seg_count = lax.axis_size("seg")
    row_count = lax.axis_size("row")
    samples = traces[0]
    channels = samples.shape[0]
    local_width = samples.shape[1]
    num_sources = sources.shape[0]
    first_sample = lax.axis_index("col") * local_width
    half_bins = NF // col_count
    sample_ids = first_sample + jnp.arange(local_width, dtype=jnp.int32)
    bin_ids = jnp.arange(half_bins * lax.axis_size("col"), dtype=jnp.int32)
    angles = turn_table(sample_ids, bin_ids, NT)
    cosine = jnp.cos(angles).astype(jnp.bfloat16)
    sine_table = jnp.sin(angles).astype(jnp.bfloat16)
    real_part = jnp.einsum("tf,ct->fc", cosine, samples, preferred_element_type=jnp.float32)
    imag_part = -jnp.einsum("tf,ct->fc", sine_table, samples, preferred_element_type=jnp.float32)
    spectra = lax.psum_scatter(
        jnp.concatenate([real_part, imag_part], axis=1).astype(jnp.bfloat16),
        "col",
        scatter_dimension=0,
        tiled=True,
    ).astype(jnp.float32)
    squares = (spectra * spectra).reshape(half_bins // BAND, BAND, 2, channels)
    band_power = jnp.sum(squares, axis=(1, 2)) / (2 * BAND) + 1e-05
    scaling = live_mask.astype(jnp.float32)[None, :] / jnp.sqrt(band_power)
    scaling = jnp.repeat(scaling, BAND, axis=0)
    whitened = (
        (spectra.reshape(half_bins, 2, channels) * scaling[:, None, :])
        .reshape(half_bins, 2 * channels)
        .astype(jnp.bfloat16)
    )
    white_real = whitened[:, :channels]
    white_imag = whitened[:, channels:]
    everyone = lax.all_gather(whitened, "row", axis=1, tiled=True)
    block_ids = sources // channels
    within = sources % channels
    real_cols = block_ids * (2 * channels) + within
    source_real = jnp.take(everyone, real_cols, axis=1)
    source_imag = jnp.take(everyone, real_cols + channels, axis=1)
    receivers = channels // (col_count * seg_count)
    bin_ids = lax.axis_index("col") * half_bins + jnp.arange(half_bins, dtype=jnp.int32)
    lag_table = lag_matrix(bin_ids)
    real_source = source_real.astype(jnp.float32)
    imag_source = source_imag.astype(jnp.float32)

    def one_group(offset):
        recv_real = lax.dynamic_slice_in_dim(white_real, offset, receivers, 1).astype(jnp.float32)
        recv_imag = lax.dynamic_slice_in_dim(white_imag, offset, receivers, 1).astype(jnp.float32)
        return correlate(recv_real, recv_imag, real_source, imag_source, lag_table)

    offsets = (
        jnp.arange(receivers * lax.axis_size(("col", "seg")) // receivers, dtype=jnp.int32)
        * receivers
    )
    blocks = lax.map(one_group, offsets)
    stacked = lax.psum_scatter(
        blocks.reshape(receivers * lax.axis_size(("col", "seg")), num_sources, LAGS).astype(
            jnp.bfloat16
        ),
        ("col", "seg"),
        scatter_dimension=0,
        tiled=True,
    ).astype(jnp.float32)
    mean_sq = jnp.mean(stacked * stacked, axis=-1, keepdims=True)
    normed = (stacked / jnp.sqrt(mean_sq + 1e-06)).astype(jnp.bfloat16)
    capacity = 3 * num_sources // row_count
    owner_ids = owners[:, 0]
    order_ids = jnp.arange(num_sources, dtype=jnp.int32)
    earlier = (owner_ids[:, None] == owner_ids[None, :]) & (order_ids[None, :] < order_ids[:, None])
    slot_rank = jnp.sum(earlier.astype(jnp.int32), axis=1)
    slot_ids = owner_ids * capacity + slot_rank
    placing = (
        jnp.arange(row_count * capacity, dtype=jnp.int32)[:, None] == slot_ids[None, :]
    ).astype(jnp.bfloat16)
    outgoing = jnp.einsum(
        "sv,gvl->sgl", placing, normed, preferred_element_type=jnp.float32
    ).astype(jnp.bfloat16)
    return lax.all_to_all(outgoing[:, None], "row", split_axis=0, concat_axis=1, tiled=True)


def host_tables(num_samples):
    samples = np.arange(num_samples, dtype=np.int64)
    bins = np.arange(NF, dtype=np.int64)
    angles = (samples[:, None] * bins[None, :] % NT) * (two_pi / NT)
    forward = np.concatenate([np.cos(angles), -np.sin(angles)], axis=1)
    lags = np.arange(LAGS, dtype=np.int64) - LAGS // 2 + NT
    lag_angles = (bins[:, None] * lags[None, :] % NT) * (two_pi / NT)
    back = np.concatenate([np.cos(lag_angles), -np.sin(lag_angles)], axis=0)
    return forward.astype(jnp.bfloat16), back.astype(jnp.bfloat16)


def at_ring(place, lines):
    second = place // lines
    return second, (1 - second) * place + second * (2 * lines - 1 - place)


def fused_kernel(
    chips, slots, traces_ref, live_ref, picking_ref, choose_ref, forward_hbm, back_ref, out_ref,
    forward, samples, given_in, picked, core_in, part, parts_in, chosen, white_source, everyone,
    cross, table_sem, pair_send, pair_recv, deal_send, deal_recv, share_send, share_recv,
    right_send, right_recv, left_send, left_recv, twin_send, twin_recv,
):
    lines = chips // 2
    half = chips // 2
    row = lax.axis_index("row")
    seg = lax.axis_index("seg")
    chip, core = row // 2, row % 2
    line, side = chip // 2, chip % 2
    place = (1 - side) * line + side * (2 * lines - 1 - line)
    channels, width = traces_ref.shape
    receivers = channels // 2
    own_sources = picking_ref.shape[0] // 2
    columns = width // chips

    def chip_at(where):
        second, first = at_ring((where + chips) % chips, lines)
        return first * 2 + second

    def remote(source, target, send_sem, recv_sem, peer):
        return pltpu.make_async_remote_copy(
            src_ref=source, dst_ref=target, send_sem=send_sem, recv_sem=recv_sem,
            device_id=peer, device_id_type=pl.DeviceIdType.MESH,
        )

    table_copy = pltpu.make_async_copy(forward_hbm, forward, table_sem)
    table_copy.start()
    twin = {"row": chip * 2 + 1 - core}
    across = {"seg": 1 - seg}
    peers = [{"row": (chip + step) % chips * 2 + core} for step in range(1, chips)]
    barrier = pltpu.get_barrier_semaphore()
    for peer in [twin, across] + peers:
        pl.semaphore_signal(barrier, inc=1, device_id=peer, device_id_type=pl.DeviceIdType.MESH)

    samples[...] = traces_ref[...] * live_ref[...]
    picked[...] = jnp.dot(
        picking_ref[...], samples[...], preferred_element_type=jnp.float32
    ).astype(picked.dtype)
    pl.semaphore_wait(barrier, chips + 1)

    def rows_of(first, count):
        return pl.ds(pl.multiple_of(first, count), count)

    my_rows = rows_of(core * own_sources, own_sources)
    twin_rows = rows_of((1 - core) * own_sources, own_sources)
    swap = remote(
        samples.at[rows_of((1 - seg) * receivers, receivers)], given_in,
        pair_send.at[0], pair_recv.at[0], across,
    )
    fold = remote(picked.at[twin_rows], core_in, pair_send.at[1], pair_recv.at[1], twin)
    fold.start()
    swap.start()

    def columns_of(which):
        return pl.ds(pl.multiple_of(which * columns, columns), columns)

    fold.wait_recv()
    part[...] = picked[my_rows, :] + core_in[...]
    deals = []
    for step, peer in enumerate(peers):
        deals.append(remote(
            part.at[:, columns_of((chip + step + 1) % chips)], parts_in.at[step],
            deal_send.at[step], deal_recv.at[step], peer,
        ))
    for copy in deals:
        copy.start()

    def whiten(traces):
        count = traces.shape[0]
        real = jnp.dot(traces, forward[:, :NF], preferred_element_type=jnp.float32)
        imag = jnp.dot(traces, forward[:, NF:], preferred_element_type=jnp.float32)
        first = lax.broadcasted_iota(jnp.int32, (2 * BAND, 2 * BAND), 0) // BAND
        second = lax.broadcasted_iota(jnp.int32, (2 * BAND, 2 * BAND), 1) // BAND
        same = jnp.where(first == second, 1.0, 0.0).astype(jnp.bfloat16)
        power = real * real + imag * imag
        scales = []
        for low in range(0, NF, 2 * BAND):
            piece = power[:, low : low + 2 * BAND]
            upper = piece.astype(jnp.bfloat16)
            lower = (piece - upper.astype(jnp.float32)).astype(jnp.bfloat16)
            total = jnp.dot(upper, same, preferred_element_type=jnp.float32) + jnp.dot(
                lower, same, preferred_element_type=jnp.float32
            )
            scales.append(lax.rsqrt(total / (2 * BAND) + 1e-05))
        scaling = jnp.concatenate(scales, axis=1)
        return (real * scaling).astype(jnp.bfloat16), (imag * scaling).astype(jnp.bfloat16)

    table_copy.wait()
    swap.wait_recv()
    kept = samples[rows_of(seg * receivers, receivers), :]
    real, imag = whiten(jnp.concatenate([kept, given_in[...]], axis=0))
    everyone[row, :, :NF] = real
    everyone[row, :, NF:] = imag

    def shard(where, stream, piece):
        return everyone.at[chip_at(where) * 2 + stream, pl.ds(piece * receivers, receivers)]

    right_peer = {"row": chip_at(place + 1) * 2 + core}
    left_peer = {"row": chip_at(place - 1) * 2 + core}

    def right(hop, piece):
        index = (hop - 1) * 2 + piece
        block = shard(place - hop + 1, core, piece)
        return remote(block, block, right_send.at[index], right_recv.at[index], right_peer)

    def left(hop, piece):
        index = (hop - 1) * 2 + piece
        block = shard(place + hop - 1, core, piece)
        return remote(block, block, left_send.at[index], left_recv.at[index], left_peer)

    order = [0]
    for hop in range(1, half):
        order += [-hop, hop]
    order.append(-half)

    def to_twin(number, piece):
        index = number * 2 + piece
        block = shard(place + order[number], core, piece)
        return remote(block, block, twin_send.at[index], twin_recv.at[index], twin)

    started = []

    def go(copy):
        copy.start()
        started.append(copy)

    for piece in range(2):
        go(right(1, piece))
        go(left(1, piece))
    for piece in range(2):
        go(to_twin(0, piece))

    for copy in deals:
        copy.wait_recv()
    total = part[:, columns_of(chip)].astype(jnp.float32)
    for step in range(chips - 1):
        total = total + parts_in[step].astype(jnp.float32)
    chosen[0, my_rows, columns_of(chip)] = total.astype(chosen.dtype)
    mine = chosen.at[0, my_rows, columns_of(chip)]
    shares = [
        remote(mine, mine, share_send.at[step], share_recv.at[step], peer)
        for step, peer in enumerate(peers)
    ]
    for copy in shares:
        copy.start()
    for copy in shares:
        copy.wait_recv()
    over = remote(
        chosen.at[0, my_rows], chosen.at[1, my_rows], pair_send.at[2], pair_recv.at[2], across
    )
    over.start()
    here = remote(
        chosen.at[0, my_rows], chosen.at[0, my_rows], pair_send.at[3], pair_recv.at[3], twin
    )
    here.start()

    def event(hop, piece):
        if hop < half or piece == 0:
            right(hop, piece).wait_recv()
            if hop + 1 < half or (hop + 1 == half and piece == 0):
                go(right(hop + 1, piece))
            go(to_twin(2 * hop - 1, piece))
        if hop < half or piece == 1:
            left(hop, piece).wait_recv()
            if hop + 1 < half or (hop + 1 == half and piece == 1):
                go(left(hop + 1, piece))
            go(to_twin(2 * hop if hop < half else 2 * hop - 1, piece))

    event(1, 0)
    over.wait_recv()
    there = remote(
        chosen.at[1, my_rows], chosen.at[1, my_rows], pair_send.at[4], pair_recv.at[4], twin
    )
    there.start()
    event(1, 1)
    here.wait_recv()
    there.wait_recv()
    choose = choose_ref[...]
    own = jnp.concatenate(
        [
            jnp.dot(choose, chosen[which], preferred_element_type=jnp.float32).astype(jnp.bfloat16)
            for which in range(2)
        ],
        axis=0,
    )
    real, imag = whiten(own)
    white_source[:, :NF] = real
    white_source[:, NF:] = imag
    padded = choose_ref.shape[0]

    def correlate_chip(number):
        for piece in range(2):
            to_twin(number, piece).wait_recv()
        where = chip_at(place + order[number])

        @pl.loop(0, 2)
        def _(stream):
            block = where * 2 + stream
            for slot in range(slots):
                cross_real = cross_imag = None
                for which in range(2):
                    rows = pl.ds(which * receivers, receivers)
                    recv_real = everyone[block, rows, :NF]
                    recv_imag = everyone[block, rows, NF:]
                    at = which * padded + slot
                    source_real = white_source[at : at + 1, :NF]
                    source_imag = white_source[at : at + 1, NF:]
                    term_real = source_real * recv_real + source_imag * recv_imag
                    term_imag = source_imag * recv_real - source_real * recv_imag
                    cross_real = term_real if cross_real is None else cross_real + term_real
                    cross_imag = term_imag if cross_imag is None else cross_imag + term_imag
                cross[slot * receivers : (slot + 1) * receivers, :NF] = cross_real
                cross[slot * receivers : (slot + 1) * receivers, NF:] = cross_imag
            stacked = jnp.dot(cross[...], back_ref[...], preferred_element_type=jnp.float32)
            mean_sq = jnp.mean(stacked * stacked, axis=-1, keepdims=True)
            normed = (stacked * lax.rsqrt(mean_sq + 1e-06)).astype(out_ref.dtype)
            for slot in range(slots):
                out_ref[slot, block] = normed[slot * receivers : (slot + 1) * receivers]

    number = 0
    for hop in range(2, half + 1):
        for piece in range(2):
            event(hop, piece)
            correlate_chip(number)
            number += 1
    while number < chips:
        correlate_chip(number)
        number += 1
    for copy in deals + shares + started + [swap, fold, over, here, there]:
        copy.wait_send()


def paired(forward, back, traces, live_mask, sources, owners):
    row_count = lax.axis_size("row")
    row = lax.axis_index("row")
    chips = row_count // 2
    channels, width = traces.shape[1:]
    receivers = channels // 2
    num_sources = sources.shape[0]
    slots = 3 * num_sources // row_count
    padded = -(-slots // 16) * 16
    owner_ids = owners[:, 0]
    order_ids = jnp.arange(num_sources, dtype=jnp.int32)
    earlier = (owner_ids[:, None] == owner_ids[None, :]) & (order_ids[None, :] < order_ids[:, None])
    rank = jnp.sum(earlier.astype(jnp.int32), axis=1)
    slot_of = jnp.where(owner_ids == row, rank, padded)
    choose = jnp.arange(padded, dtype=jnp.int32)[:, None] == slot_of[None, :]
    local_ids = row * channels + jnp.arange(channels, dtype=jnp.int32)
    picking = sources[:, None] == local_ids[None, :]
    kind = traces.dtype
    whole = pl.BlockSpec(memory_space=pltpu.VMEM)
    dma = pltpu.SemaphoreType.DMA
    hops = chips // 2 * 2
    return pl.pallas_call(
        partial(fused_kernel, chips, slots),
        in_specs=[whole] * 4 + [pl.BlockSpec(memory_space=pl.ANY), whole],
        out_specs=whole,
        out_shape=jax.ShapeDtypeStruct((slots, row_count, receivers, LAGS), jnp.bfloat16),
        scratch_shapes=[
            pltpu.VMEM(forward.shape, kind),
            pltpu.VMEM((channels, width), kind),
            pltpu.VMEM((receivers, width), kind),
            pltpu.VMEM((num_sources, width), kind),
            pltpu.VMEM((num_sources // 2, width), kind),
            pltpu.VMEM((num_sources // 2, width), kind),
            pltpu.VMEM((chips - 1, num_sources // 2, width // chips), kind),
            pltpu.VMEM((2, num_sources, width), kind),
            pltpu.VMEM((2 * padded, 2 * NF), kind),
            pltpu.VMEM((row_count, channels, 2 * NF), kind),
            pltpu.VMEM((slots * receivers, 2 * NF), kind),
            dma,
            dma((5,)), dma((5,)),
            dma((chips - 1,)), dma((chips - 1,)),
            dma((chips - 1,)), dma((chips - 1,)),
            dma((hops,)), dma((hops,)),
            dma((hops,)), dma((hops,)),
            dma((2 * chips,)), dma((2 * chips,)),
        ],
        compiler_params=pltpu.CompilerParams(
            collective_id=0, has_side_effects=True, vmem_limit_bytes=56 << 20
        ),
        cost_estimate=pl.CostEstimate(
            flops=2 * slots * row_count * receivers * 2 * NF * LAGS,
            bytes_accessed=2 * width * 2 * NF,
            transcendentals=0,
        ),
    )(traces[0], live_mask.astype(kind)[:, None], picking.astype(kind), choose.astype(kind),
      forward, back)


def solution(mesh):
    placed = (P(("run", "seg"), "row", "col"), P(("run", "row")), P(), P())
    body = local
    if mesh.shape["col"] == 1 and mesh.shape["seg"] == 2 and mesh.shape["row"] % 4 == 0:
        forward, back = host_tables(NT)
        body = partial(paired, forward, back)
    return jax.shard_map(
        body,
        mesh=mesh,
        in_specs=placed,
        out_specs=P(("run", "row"), None, ("col", "seg"), None),
        check_vma=False,
    )
```

```python
import math
from functools import partial

import jax
import jax.numpy as jnp
import numpy as np
from jax import lax
from jax.experimental import pallas as pl
from jax.experimental.pallas import tpu as pltpu
from jax.sharding import PartitionSpec as P

NT = 2048
NF = 1024
LAGS = 256
BAND = 64


two_pi = 2.0 * math.pi


def turn_table(first_ids, second_ids, period):
    product = first_ids[:, None] * second_ids[None, :] % period
    return product.astype(jnp.float32) * (two_pi / period)


def lag_matrix(bin_ids):
    lag_ids = jnp.arange(LAGS, dtype=jnp.int32) - LAGS // 2 + NT
    lag_angles = turn_table(bin_ids, lag_ids, NT)
    return jnp.concatenate(
        [jnp.cos(lag_angles).astype(jnp.bfloat16), -jnp.sin(lag_angles).astype(jnp.bfloat16)],
        axis=0,
    )


def correlate(recv_real, recv_imag, real_source, imag_source, lag_table):
    cross_real = (
        real_source[:, None, :] * recv_real[:, :, None]
        + imag_source[:, None, :] * recv_imag[:, :, None]
    ).astype(jnp.bfloat16)
    cross_imag = (
        imag_source[:, None, :] * recv_real[:, :, None]
        - real_source[:, None, :] * recv_imag[:, :, None]
    ).astype(jnp.bfloat16)
    stacked_cross = jnp.concatenate([cross_real, cross_imag], axis=0)
    return jnp.einsum("fl,fgv->gvl", lag_table, stacked_cross, preferred_element_type=jnp.float32)


def local(traces, live_mask, sources, owners):
    col_count = lax.axis_size("col")
    seg_count = lax.axis_size("seg")
    row_count = lax.axis_size("row")
    samples = traces[0]
    channels = samples.shape[0]
    local_width = samples.shape[1]
    num_sources = sources.shape[0]
    first_sample = lax.axis_index("col") * local_width
    half_bins = NF // col_count
    sample_ids = first_sample + jnp.arange(local_width, dtype=jnp.int32)
    bin_ids = jnp.arange(half_bins * lax.axis_size("col"), dtype=jnp.int32)
    angles = turn_table(sample_ids, bin_ids, NT)
    cosine = jnp.cos(angles).astype(jnp.bfloat16)
    sine_table = jnp.sin(angles).astype(jnp.bfloat16)
    real_part = jnp.einsum("tf,ct->fc", cosine, samples, preferred_element_type=jnp.float32)
    imag_part = -jnp.einsum("tf,ct->fc", sine_table, samples, preferred_element_type=jnp.float32)
    spectra = lax.psum_scatter(
        jnp.concatenate([real_part, imag_part], axis=1).astype(jnp.bfloat16),
        "col",
        scatter_dimension=0,
        tiled=True,
    ).astype(jnp.float32)
    squares = (spectra * spectra).reshape(half_bins // BAND, BAND, 2, channels)
    band_power = jnp.sum(squares, axis=(1, 2)) / (2 * BAND) + 1e-05
    scaling = live_mask.astype(jnp.float32)[None, :] / jnp.sqrt(band_power)
    scaling = jnp.repeat(scaling, BAND, axis=0)
    whitened = (
        (spectra.reshape(half_bins, 2, channels) * scaling[:, None, :])
        .reshape(half_bins, 2 * channels)
        .astype(jnp.bfloat16)
    )
    white_real = whitened[:, :channels]
    white_imag = whitened[:, channels:]
    everyone = lax.all_gather(whitened, "row", axis=1, tiled=True)
    block_ids = sources // channels
    within = sources % channels
    real_cols = block_ids * (2 * channels) + within
    source_real = jnp.take(everyone, real_cols, axis=1)
    source_imag = jnp.take(everyone, real_cols + channels, axis=1)
    receivers = channels // (col_count * seg_count)
    bin_ids = lax.axis_index("col") * half_bins + jnp.arange(half_bins, dtype=jnp.int32)
    lag_table = lag_matrix(bin_ids)
    real_source = source_real.astype(jnp.float32)
    imag_source = source_imag.astype(jnp.float32)

    def one_group(offset):
        recv_real = lax.dynamic_slice_in_dim(white_real, offset, receivers, 1).astype(jnp.float32)
        recv_imag = lax.dynamic_slice_in_dim(white_imag, offset, receivers, 1).astype(jnp.float32)
        return correlate(recv_real, recv_imag, real_source, imag_source, lag_table)

    offsets = (
        jnp.arange(receivers * lax.axis_size(("col", "seg")) // receivers, dtype=jnp.int32)
        * receivers
    )
    blocks = lax.map(one_group, offsets)
    stacked = lax.psum_scatter(
        blocks.reshape(receivers * lax.axis_size(("col", "seg")), num_sources, LAGS).astype(
            jnp.bfloat16
        ),
        ("col", "seg"),
        scatter_dimension=0,
        tiled=True,
    ).astype(jnp.float32)
    mean_sq = jnp.mean(stacked * stacked, axis=-1, keepdims=True)
    normed = (stacked / jnp.sqrt(mean_sq + 1e-06)).astype(jnp.bfloat16)
    capacity = 3 * num_sources // row_count
    owner_ids = owners[:, 0]
    order_ids = jnp.arange(num_sources, dtype=jnp.int32)
    earlier = (owner_ids[:, None] == owner_ids[None, :]) & (order_ids[None, :] < order_ids[:, None])
    slot_rank = jnp.sum(earlier.astype(jnp.int32), axis=1)
    slot_ids = owner_ids * capacity + slot_rank
    placing = (
        jnp.arange(row_count * capacity, dtype=jnp.int32)[:, None] == slot_ids[None, :]
    ).astype(jnp.bfloat16)
    outgoing = jnp.einsum(
        "sv,gvl->sgl", placing, normed, preferred_element_type=jnp.float32
    ).astype(jnp.bfloat16)
    return lax.all_to_all(outgoing[:, None], "row", split_axis=0, concat_axis=1, tiled=True)


def host_tables(num_samples):
    samples = np.arange(num_samples, dtype=np.int64)
    bins = np.arange(NF, dtype=np.int64)
    angles = (samples[:, None] * bins[None, :] % NT) * (two_pi / NT)
    forward = np.concatenate([np.cos(angles), -np.sin(angles)], axis=1)
    lags = np.arange(LAGS, dtype=np.int64) - LAGS // 2 + NT
    lag_angles = (bins[:, None] * lags[None, :] % NT) * (two_pi / NT)
    back = np.concatenate([np.cos(lag_angles), -np.sin(lag_angles)], axis=0)
    return forward.astype(jnp.bfloat16), back.astype(jnp.bfloat16)


def at_ring(place, lines):
    second = place // lines
    return second, (1 - second) * place + second * (2 * lines - 1 - place)


def fused_kernel(
    chips, slots, traces_ref, live_ref, sources_ref, owners_ref, forward_hbm, back_ref, out_hbm,
    forward, samples, given_in, picked, core_in, part, parts_in, chosen, white_source, everyone,
    cross_even, cross_odd, finished, table_sem, out_sem, pair_send, pair_recv, deal_send, deal_recv, share_send, share_recv,
    right_send, right_recv, left_send, left_recv, twin_send, twin_recv,
):
    lines = chips // 2
    half = chips // 2
    row = lax.axis_index("row")
    seg = lax.axis_index("seg")
    chip, core = row // 2, row % 2
    line, side = chip // 2, chip % 2
    place = (1 - side) * line + side * (2 * lines - 1 - line)
    channels, width = traces_ref.shape
    receivers = channels // 2
    num_sources = sources_ref.shape[1]
    own_sources = num_sources // 2
    padded = white_source.shape[0] // 2
    columns = width // chips

    def chip_at(where):
        second, first = at_ring((where + chips) % chips, lines)
        return first * 2 + second

    def remote(source, target, send_sem, recv_sem, peer):
        return pltpu.make_async_remote_copy(
            src_ref=source, dst_ref=target, send_sem=send_sem, recv_sem=recv_sem,
            device_id=peer, device_id_type=pl.DeviceIdType.MESH,
        )

    table_copy = pltpu.make_async_copy(forward_hbm, forward, table_sem)
    table_copy.start()
    twin = {"row": chip * 2 + 1 - core}
    across = {"seg": 1 - seg}
    peers = [{"row": (chip + step) % chips * 2 + core} for step in range(1, chips)]
    barrier = pltpu.get_barrier_semaphore()
    for peer in [twin, across] + peers:
        pl.semaphore_signal(barrier, inc=1, device_id=peer, device_id_type=pl.DeviceIdType.MESH)

    def ids(shape, axis):
        return lax.broadcasted_iota(jnp.int32, shape, axis).astype(jnp.float32)

    def column(values):
        square = (values.shape[1], values.shape[1])
        kept_ones = jnp.where(ids(square, 0) == ids(square, 1), values, 0.0)
        return jnp.sum(kept_ones, axis=1, keepdims=True)

    live = live_ref[...].astype(jnp.float32)
    source_row = sources_ref[...].astype(jnp.float32)
    owner_row = owners_ref[...].astype(jnp.float32)
    my_row = row.astype(jnp.float32)
    samples[...] = traces_ref[...] * column(live).astype(traces_ref.dtype)
    local_ids = ids((num_sources, channels), 1) + my_row * channels
    picking = jnp.where(column(source_row) == local_ids, 1.0, 0.0).astype(samples.dtype)
    picked[...] = jnp.dot(
        picking, samples[...], preferred_element_type=jnp.float32
    ).astype(picked.dtype)
    square = (num_sources, num_sources)
    earlier = jnp.where(ids(square, 0) < ids(square, 1), 1.0, 0.0)
    alike = jnp.where(column(owner_row) == owner_row, earlier, 0.0)
    rank = jnp.sum(alike, axis=0, keepdims=True)
    slot_of = jnp.where(owner_row == my_row, rank, float(padded))
    choose = jnp.where(ids((padded, num_sources), 0) == slot_of, 1.0, 0.0).astype(samples.dtype)
    pl.semaphore_wait(barrier, chips + 1)

    def rows_of(first, count):
        return pl.ds(pl.multiple_of(first, count), count)

    my_rows = rows_of(core * own_sources, own_sources)
    twin_rows = rows_of((1 - core) * own_sources, own_sources)
    swap = remote(
        samples.at[rows_of((1 - seg) * receivers, receivers)], given_in,
        pair_send.at[0], pair_recv.at[0], across,
    )
    fold = remote(picked.at[twin_rows], core_in, pair_send.at[1], pair_recv.at[1], twin)
    fold.start()
    swap.start()

    def columns_of(which):
        return pl.ds(pl.multiple_of(which * columns, columns), columns)

    fold.wait_recv()
    part[...] = picked[my_rows, :] + core_in[...]
    deals = []
    for step, peer in enumerate(peers):
        deals.append(remote(
            part.at[:, columns_of((chip + step + 1) % chips)], parts_in.at[step],
            deal_send.at[step], deal_recv.at[step], peer,
        ))
    for copy in deals:
        copy.start()

    def whiten(traces):
        count = traces.shape[0]
        real = jnp.dot(traces, forward[:, :NF], preferred_element_type=jnp.float32)
        imag = jnp.dot(traces, forward[:, NF:], preferred_element_type=jnp.float32)
        first = lax.broadcasted_iota(jnp.int32, (2 * BAND, 2 * BAND), 0) // BAND
        second = lax.broadcasted_iota(jnp.int32, (2 * BAND, 2 * BAND), 1) // BAND
        same = jnp.where(first == second, 1.0, 0.0).astype(jnp.bfloat16)
        power = real * real + imag * imag
        scales = []
        for low in range(0, NF, 2 * BAND):
            piece = power[:, low : low + 2 * BAND]
            upper = piece.astype(jnp.bfloat16)
            lower = (piece - upper.astype(jnp.float32)).astype(jnp.bfloat16)
            total = jnp.dot(upper, same, preferred_element_type=jnp.float32) + jnp.dot(
                lower, same, preferred_element_type=jnp.float32
            )
            scales.append(lax.rsqrt(total / (2 * BAND) + 1e-05))
        scaling = jnp.concatenate(scales, axis=1)
        return (real * scaling).astype(jnp.bfloat16), (imag * scaling).astype(jnp.bfloat16)

    table_copy.wait()
    swap.wait_recv()
    kept = samples[rows_of(seg * receivers, receivers), :]
    real, imag = whiten(jnp.concatenate([kept, given_in[...]], axis=0))
    everyone[row, :, :NF] = real
    everyone[row, :, NF:] = imag

    def shard(where, stream, piece):
        return everyone.at[chip_at(where) * 2 + stream, pl.ds(piece * receivers, receivers)]

    right_peer = {"row": chip_at(place + 1) * 2 + core}
    left_peer = {"row": chip_at(place - 1) * 2 + core}

    def right(hop, piece):
        index = (hop - 1) * 2 + piece
        block = shard(place - hop + 1, core, piece)
        return remote(block, block, right_send.at[index], right_recv.at[index], right_peer)

    def left(hop, piece):
        index = (hop - 1) * 2 + piece
        block = shard(place + hop - 1, core, piece)
        return remote(block, block, left_send.at[index], left_recv.at[index], left_peer)

    order = [0]
    for hop in range(1, half):
        order += [-hop, hop]
    order.append(-half)

    def to_twin(number, piece):
        index = number * 2 + piece
        block = shard(place + order[number], core, piece)
        return remote(block, block, twin_send.at[index], twin_recv.at[index], twin)

    started = []

    def go(copy):
        copy.start()
        started.append(copy)

    for piece in range(2):
        go(right(1, piece))
        go(left(1, piece))
    for piece in range(2):
        go(to_twin(0, piece))

    for copy in deals:
        copy.wait_recv()
    total = part[:, columns_of(chip)].astype(jnp.float32)
    for step in range(chips - 1):
        total = total + parts_in[step].astype(jnp.float32)
    chosen[0, my_rows, columns_of(chip)] = total.astype(chosen.dtype)
    mine = chosen.at[0, my_rows, columns_of(chip)]
    shares = [
        remote(mine, mine, share_send.at[step], share_recv.at[step], peer)
        for step, peer in enumerate(peers)
    ]
    for copy in shares:
        copy.start()
    for copy in shares:
        copy.wait_recv()
    over = remote(
        chosen.at[0, my_rows], chosen.at[1, my_rows], pair_send.at[2], pair_recv.at[2], across
    )
    over.start()
    here = remote(
        chosen.at[0, my_rows], chosen.at[0, my_rows], pair_send.at[3], pair_recv.at[3], twin
    )
    here.start()

    def event(hop, piece):
        if hop < half or piece == 0:
            right(hop, piece).wait_recv()
            if hop + 1 < half or (hop + 1 == half and piece == 0):
                go(right(hop + 1, piece))
            go(to_twin(2 * hop - 1, piece))
        if hop < half or piece == 1:
            left(hop, piece).wait_recv()
            if hop + 1 < half or (hop + 1 == half and piece == 1):
                go(left(hop + 1, piece))
            go(to_twin(2 * hop if hop < half else 2 * hop - 1, piece))

    event(1, 0)
    event(1, 1)
    over.wait_recv()
    there = remote(
        chosen.at[1, my_rows], chosen.at[1, my_rows], pair_send.at[4], pair_recv.at[4], twin
    )
    there.start()
    here.wait_recv()
    event(2, 0)
    there.wait_recv()
    own = jnp.concatenate(
        [
            jnp.dot(choose, chosen[which], preferred_element_type=jnp.float32).astype(jnp.bfloat16)
            for which in range(2)
        ],
        axis=0,
    )
    real, imag = whiten(own)
    white_source[:, :NF] = real
    white_source[:, NF:] = imag

    def cross_block(block, cross):
        for slot in range(slots):
            cross_real = cross_imag = None
            for which in range(2):
                rows = pl.ds(which * receivers, receivers)
                recv_real = everyone[block, rows, :NF]
                recv_imag = everyone[block, rows, NF:]
                at = which * padded + slot
                source_real = white_source[at : at + 1, :NF]
                source_imag = white_source[at : at + 1, NF:]
                term_real = source_real * recv_real + source_imag * recv_imag
                term_imag = source_imag * recv_real - source_real * recv_imag
                cross_real = term_real if cross_real is None else cross_real + term_real
                cross_imag = term_imag if cross_imag is None else cross_imag + term_imag
            cross[slot * receivers : (slot + 1) * receivers, :NF] = cross_real
            cross[slot * receivers : (slot + 1) * receivers, NF:] = cross_imag

    def finish_block(block, cross, index):
        stacked = jnp.dot(cross[...], back_ref[...], preferred_element_type=jnp.float32)
        mean_sq = jnp.mean(stacked * stacked, axis=-1, keepdims=True)
        normed = (stacked * lax.rsqrt(mean_sq + 1e-06)).astype(finished.dtype)
        for slot in range(slots):
            finished[block, slot] = normed[slot * receivers : (slot + 1) * receivers]
        copy = pltpu.make_async_copy(finished.at[block], out_hbm.at[:, block], out_sem.at[index])
        copy.start()
        written.append(copy)

    written = []
    waiting = []

    def finish_waiting():
        while waiting:
            finish_block(*waiting.pop())

    def correlate_chip(number):
        for piece in range(2):
            to_twin(number, piece).wait_recv()
        where = chip_at(place + order[number])
        for stream, cross in enumerate((cross_even, cross_odd)):
            block = where * 2 + stream
            finish_waiting()
            cross_block(block, cross)
            waiting.append((block, cross, number * 2 + stream))

    event(2, 1)
    correlate_chip(0)
    number = 1
    for hop in range(3, half + 1):
        for piece in range(2):
            event(hop, piece)
            correlate_chip(number)
            number += 1
    while number < chips:
        correlate_chip(number)
        number += 1
    finish_waiting()
    for copy in deals + shares + started + [swap, fold, over, here, there]:
        copy.wait_send()
    for copy in written:
        copy.wait()


def paired(forward, back, traces, live_mask, sources, owners):
    row_count = lax.axis_size("row")
    chips = row_count // 2
    channels, width = traces.shape[1:]
    receivers = channels // 2
    num_sources = sources.shape[0]
    slots = 3 * num_sources // row_count
    padded = -(-slots // 16) * 16
    kind = traces.dtype
    whole = pl.BlockSpec(memory_space=pltpu.VMEM)
    dma = pltpu.SemaphoreType.DMA
    hops = chips // 2 * 2
    return pl.pallas_call(
        partial(fused_kernel, chips, slots),
        in_specs=[whole] * 4 + [pl.BlockSpec(memory_space=pltpu.HBM), whole],
        out_specs=pl.BlockSpec(memory_space=pl.ANY),
        out_shape=jax.ShapeDtypeStruct((slots, row_count, receivers, LAGS), jnp.bfloat16),
        scratch_shapes=[
            pltpu.VMEM(forward.shape, kind),
            pltpu.VMEM((channels, width), kind),
            pltpu.VMEM((receivers, width), kind),
            pltpu.VMEM((num_sources, width), kind),
            pltpu.VMEM((num_sources // 2, width), kind),
            pltpu.VMEM((num_sources // 2, width), kind),
            pltpu.VMEM((chips - 1, num_sources // 2, width // chips), kind),
            pltpu.VMEM((2, num_sources, width), kind),
            pltpu.VMEM((2 * padded, 2 * NF), kind),
            pltpu.VMEM((row_count, channels, 2 * NF), kind),
            pltpu.VMEM((slots * receivers, 2 * NF), kind),
            pltpu.VMEM((slots * receivers, 2 * NF), kind),
            pltpu.VMEM((row_count, slots, receivers, LAGS), kind),
            dma,
            dma((row_count,)),
            dma((5,)), dma((5,)),
            dma((chips - 1,)), dma((chips - 1,)),
            dma((chips - 1,)), dma((chips - 1,)),
            dma((hops,)), dma((hops,)),
            dma((hops,)), dma((hops,)),
            dma((2 * chips,)), dma((2 * chips,)),
        ],
        compiler_params=pltpu.CompilerParams(
            collective_id=0, has_side_effects=True, vmem_limit_bytes=30 << 20
        ),
        cost_estimate=pl.CostEstimate(
            flops=2 * slots * row_count * receivers * 2 * NF * LAGS,
            bytes_accessed=2 * width * 2 * NF,
            transcendentals=0,
        ),
    )(traces[0], live_mask[None, :], sources[None, :], owners.reshape(1, num_sources), forward, back)


def solution(mesh):
    placed = (P(("run", "seg"), "row", "col"), P(("run", "row")), P(), P())
    body = local
    if mesh.shape["col"] == 1 and mesh.shape["seg"] == 2 and mesh.shape["row"] % 4 == 0:
        forward, back = host_tables(NT)
        body = partial(paired, forward, back)
    return jax.shard_map(
        body,
        mesh=mesh,
        in_specs=placed,
        out_specs=P(("run", "row"), None, ("col", "seg"), None),
        check_vma=False,
    )
```

```python
import math
from functools import partial

import jax
import jax.numpy as jnp
import numpy as np
from jax import lax
from jax.experimental import pallas as pl
from jax.experimental.pallas import tpu as pltpu
from jax.sharding import PartitionSpec as P

NT = 2048
NF = 1024
LAGS = 256
BAND = 64


two_pi = 2.0 * math.pi


def turn_table(first_ids, second_ids, period):
    product = first_ids[:, None] * second_ids[None, :] % period
    return product.astype(jnp.float32) * (two_pi / period)


def lag_matrix(bin_ids):
    lag_ids = jnp.arange(LAGS, dtype=jnp.int32) - LAGS // 2 + NT
    lag_angles = turn_table(bin_ids, lag_ids, NT)
    return jnp.concatenate(
        [jnp.cos(lag_angles).astype(jnp.bfloat16), -jnp.sin(lag_angles).astype(jnp.bfloat16)],
        axis=0,
    )


def correlate(recv_real, recv_imag, real_source, imag_source, lag_table):
    cross_real = (
        real_source[:, None, :] * recv_real[:, :, None]
        + imag_source[:, None, :] * recv_imag[:, :, None]
    ).astype(jnp.bfloat16)
    cross_imag = (
        imag_source[:, None, :] * recv_real[:, :, None]
        - real_source[:, None, :] * recv_imag[:, :, None]
    ).astype(jnp.bfloat16)
    stacked_cross = jnp.concatenate([cross_real, cross_imag], axis=0)
    return jnp.einsum("fl,fgv->gvl", lag_table, stacked_cross, preferred_element_type=jnp.float32)


def local(traces, live_mask, sources, owners):
    col_count = lax.axis_size("col")
    seg_count = lax.axis_size("seg")
    row_count = lax.axis_size("row")
    samples = traces[0]
    channels = samples.shape[0]
    local_width = samples.shape[1]
    num_sources = sources.shape[0]
    first_sample = lax.axis_index("col") * local_width
    half_bins = NF // col_count
    sample_ids = first_sample + jnp.arange(local_width, dtype=jnp.int32)
    bin_ids = jnp.arange(half_bins * lax.axis_size("col"), dtype=jnp.int32)
    angles = turn_table(sample_ids, bin_ids, NT)
    cosine = jnp.cos(angles).astype(jnp.bfloat16)
    sine_table = jnp.sin(angles).astype(jnp.bfloat16)
    real_part = jnp.einsum("tf,ct->fc", cosine, samples, preferred_element_type=jnp.float32)
    imag_part = -jnp.einsum("tf,ct->fc", sine_table, samples, preferred_element_type=jnp.float32)
    spectra = lax.psum_scatter(
        jnp.concatenate([real_part, imag_part], axis=1).astype(jnp.bfloat16),
        "col",
        scatter_dimension=0,
        tiled=True,
    ).astype(jnp.float32)
    squares = (spectra * spectra).reshape(half_bins // BAND, BAND, 2, channels)
    band_power = jnp.sum(squares, axis=(1, 2)) / (2 * BAND) + 1e-05
    scaling = live_mask.astype(jnp.float32)[None, :] / jnp.sqrt(band_power)
    scaling = jnp.repeat(scaling, BAND, axis=0)
    whitened = (
        (spectra.reshape(half_bins, 2, channels) * scaling[:, None, :])
        .reshape(half_bins, 2 * channels)
        .astype(jnp.bfloat16)
    )
    white_real = whitened[:, :channels]
    white_imag = whitened[:, channels:]
    everyone = lax.all_gather(whitened, "row", axis=1, tiled=True)
    block_ids = sources // channels
    within = sources % channels
    real_cols = block_ids * (2 * channels) + within
    source_real = jnp.take(everyone, real_cols, axis=1)
    source_imag = jnp.take(everyone, real_cols + channels, axis=1)
    receivers = channels // (col_count * seg_count)
    bin_ids = lax.axis_index("col") * half_bins + jnp.arange(half_bins, dtype=jnp.int32)
    lag_table = lag_matrix(bin_ids)
    real_source = source_real.astype(jnp.float32)
    imag_source = source_imag.astype(jnp.float32)

    def one_group(offset):
        recv_real = lax.dynamic_slice_in_dim(white_real, offset, receivers, 1).astype(jnp.float32)
        recv_imag = lax.dynamic_slice_in_dim(white_imag, offset, receivers, 1).astype(jnp.float32)
        return correlate(recv_real, recv_imag, real_source, imag_source, lag_table)

    offsets = (
        jnp.arange(receivers * lax.axis_size(("col", "seg")) // receivers, dtype=jnp.int32)
        * receivers
    )
    blocks = lax.map(one_group, offsets)
    stacked = lax.psum_scatter(
        blocks.reshape(receivers * lax.axis_size(("col", "seg")), num_sources, LAGS).astype(
            jnp.bfloat16
        ),
        ("col", "seg"),
        scatter_dimension=0,
        tiled=True,
    ).astype(jnp.float32)
    mean_sq = jnp.mean(stacked * stacked, axis=-1, keepdims=True)
    normed = (stacked / jnp.sqrt(mean_sq + 1e-06)).astype(jnp.bfloat16)
    capacity = 3 * num_sources // row_count
    owner_ids = owners[:, 0]
    order_ids = jnp.arange(num_sources, dtype=jnp.int32)
    earlier = (owner_ids[:, None] == owner_ids[None, :]) & (order_ids[None, :] < order_ids[:, None])
    slot_rank = jnp.sum(earlier.astype(jnp.int32), axis=1)
    slot_ids = owner_ids * capacity + slot_rank
    placing = (
        jnp.arange(row_count * capacity, dtype=jnp.int32)[:, None] == slot_ids[None, :]
    ).astype(jnp.bfloat16)
    outgoing = jnp.einsum(
        "sv,gvl->sgl", placing, normed, preferred_element_type=jnp.float32
    ).astype(jnp.bfloat16)
    return lax.all_to_all(outgoing[:, None], "row", split_axis=0, concat_axis=1, tiled=True)


def host_tables(num_samples):
    samples = np.arange(num_samples, dtype=np.int64)
    bins = np.arange(NF, dtype=np.int64)
    angles = (samples[:, None] * bins[None, :] % NT) * (two_pi / NT)
    forward = np.concatenate([np.cos(angles), -np.sin(angles)], axis=1)
    lags = np.arange(LAGS, dtype=np.int64) - LAGS // 2 + NT
    lag_angles = (bins[:, None] * lags[None, :] % NT) * (two_pi / NT)
    back = np.concatenate([np.cos(lag_angles), -np.sin(lag_angles)], axis=0)
    return forward.astype(jnp.bfloat16), back.astype(jnp.bfloat16)


def at_ring(place, lines):
    second = place // lines
    return second, (1 - second) * place + second * (2 * lines - 1 - place)


def fused_kernel(
    chips, slots, traces_hbm, live_hbm, sources_hbm, owners_hbm, forward_hbm, back_hbm, out_hbm,
    traces_ref, live_ref, sources_ref, owners_ref, back_ref, in_sem, forward, samples, given_in, picked, core_in, part, parts_in, chosen, white_source, everyone,
    cross_even, cross_odd, joined, own, finished, table_sem, out_sem, pair_send, pair_recv, deal_send, deal_recv, share_send, share_recv,
    right_send, right_recv, left_send, left_recv, twin_send, twin_recv,
):
    lines = chips // 2
    half = chips // 2
    row = lax.axis_index("row")
    seg = lax.axis_index("seg")
    chip, core = row // 2, row % 2
    line, side = chip // 2, chip % 2
    place = (1 - side) * line + side * (2 * lines - 1 - line)
    channels, width = traces_ref.shape
    receivers = channels // 2
    num_sources = sources_ref.shape[1]
    own_sources = num_sources // 2
    padded = white_source.shape[0] // 2
    columns = width // chips

    def chip_at(where):
        second, first = at_ring((where + chips) % chips, lines)
        return first * 2 + second

    def remote(source, target, send_sem, recv_sem, peer):
        return pltpu.make_async_remote_copy(
            src_ref=source, dst_ref=target, send_sem=send_sem, recv_sem=recv_sem,
            device_id=peer, device_id_type=pl.DeviceIdType.MESH,
        )

    inputs = [
        pltpu.make_async_copy(source, target, in_sem.at[index])
        for index, (source, target) in enumerate((
            (sources_hbm, sources_ref), (owners_hbm, owners_ref), (live_hbm, live_ref),
            (traces_hbm, traces_ref), (back_hbm, back_ref),
        ))
    ]
    for copy in inputs:
        copy.start()
    table_copy = pltpu.make_async_copy(forward_hbm, forward, table_sem)
    table_copy.start()
    twin = {"row": chip * 2 + 1 - core}
    across = {"seg": 1 - seg}
    peers = [{"row": (chip + step) % chips * 2 + core} for step in range(1, chips)]
    barrier = pltpu.get_barrier_semaphore()
    for peer in [twin, across] + peers:
        pl.semaphore_signal(barrier, inc=1, device_id=peer, device_id_type=pl.DeviceIdType.MESH)

    for copy in inputs:
        copy.wait()

    def ids(shape, axis):
        return lax.broadcasted_iota(jnp.int32, shape, axis).astype(jnp.float32)

    def column(values):
        square = (values.shape[1], values.shape[1])
        kept_ones = jnp.where(ids(square, 0) == ids(square, 1), values, 0.0)
        return jnp.sum(kept_ones, axis=1, keepdims=True)

    live = live_ref[...].astype(jnp.float32)
    source_row = sources_ref[...].astype(jnp.float32)
    owner_row = owners_ref[...].astype(jnp.float32)
    my_row = row.astype(jnp.float32)
    samples[...] = traces_ref[...] * column(live).astype(traces_ref.dtype)
    local_ids = ids((num_sources, channels), 1) + my_row * channels
    picking = jnp.where(column(source_row) == local_ids, 1.0, 0.0).astype(samples.dtype)
    picked[...] = jnp.dot(
        picking, samples[...], preferred_element_type=jnp.float32
    ).astype(picked.dtype)
    square = (num_sources, num_sources)
    earlier = jnp.where(ids(square, 0) < ids(square, 1), 1.0, 0.0)
    alike = jnp.where(column(owner_row) == owner_row, earlier, 0.0)
    rank = jnp.sum(alike, axis=0, keepdims=True)
    slot_of = jnp.where(owner_row == my_row, rank, float(padded))
    choose = jnp.where(ids((padded, num_sources), 0) == slot_of, 1.0, 0.0).astype(samples.dtype)
    pl.semaphore_wait(barrier, chips + 1)

    def rows_of(first, count):
        return pl.ds(pl.multiple_of(first, count), count)

    my_rows = rows_of(core * own_sources, own_sources)
    twin_rows = rows_of((1 - core) * own_sources, own_sources)
    swap = remote(
        samples.at[rows_of((1 - seg) * receivers, receivers)], given_in,
        pair_send.at[0], pair_recv.at[0], across,
    )
    fold = remote(picked.at[twin_rows], core_in, pair_send.at[1], pair_recv.at[1], twin)
    fold.start()
    swap.start()

    def columns_of(which):
        return pl.ds(pl.multiple_of(which * columns, columns), columns)

    fold.wait_recv()
    part[...] = picked[my_rows, :] + core_in[...]
    deals = []
    for step, peer in enumerate(peers):
        deals.append(remote(
            part.at[:, columns_of((chip + step + 1) % chips)], parts_in.at[step],
            deal_send.at[step], deal_recv.at[step], peer,
        ))
    for copy in deals:
        copy.start()

    chunk = 4 * BAND

    def whiten(traces, target):
        first = lax.broadcasted_iota(jnp.int32, (chunk, chunk), 0) // BAND
        second = lax.broadcasted_iota(jnp.int32, (chunk, chunk), 1) // BAND
        same = jnp.where(first == second, 1.0, 0.0).astype(jnp.bfloat16)

        @pl.loop(0, NF // chunk)
        def _(step):
            low = pl.ds(pl.multiple_of(step * chunk, chunk), chunk)
            high = pl.ds(pl.multiple_of(NF + step * chunk, chunk), chunk)
            real = jnp.dot(traces[...], forward[:, low], preferred_element_type=jnp.float32)
            imag = jnp.dot(traces[...], forward[:, high], preferred_element_type=jnp.float32)
            power = real * real + imag * imag
            upper = power.astype(jnp.bfloat16)
            lower = (power - upper.astype(jnp.float32)).astype(jnp.bfloat16)
            total = jnp.dot(upper, same, preferred_element_type=jnp.float32) + jnp.dot(
                lower, same, preferred_element_type=jnp.float32
            )
            scaling = lax.rsqrt(total / (2 * BAND) + 1e-05)
            target[:, low] = (real * scaling).astype(jnp.bfloat16)
            target[:, high] = (imag * scaling).astype(jnp.bfloat16)

    table_copy.wait()
    swap.wait_recv()
    joined[:receivers] = samples[rows_of(seg * receivers, receivers), :]
    joined[receivers:] = given_in[...]
    whiten(joined, everyone.at[row])

    def shard(where, stream, piece):
        return everyone.at[chip_at(where) * 2 + stream, pl.ds(piece * receivers, receivers)]

    right_peer = {"row": chip_at(place + 1) * 2 + core}
    left_peer = {"row": chip_at(place - 1) * 2 + core}

    def right(hop, piece):
        index = (hop - 1) * 2 + piece
        block = shard(place - hop + 1, core, piece)
        return remote(block, block, right_send.at[index], right_recv.at[index], right_peer)

    def left(hop, piece):
        index = (hop - 1) * 2 + piece
        block = shard(place + hop - 1, core, piece)
        return remote(block, block, left_send.at[index], left_recv.at[index], left_peer)

    def offset_of(number):
        return (number + 1) // 2 * (1 - 2 * (number % 2))

    def to_twin(number, piece):
        index = number * 2 + piece
        block = shard(place + offset_of(number), core, piece)
        return remote(block, block, twin_send.at[index], twin_recv.at[index], twin)

    for piece in range(2):
        right(1, piece).start()
        left(1, piece).start()
    for piece in range(2):
        to_twin(0, piece).start()

    for copy in deals:
        copy.wait_recv()
    total = part[:, columns_of(chip)].astype(jnp.float32)
    for step in range(chips - 1):
        total = total + parts_in[step].astype(jnp.float32)
    chosen[0, my_rows, columns_of(chip)] = total.astype(chosen.dtype)
    mine = chosen.at[0, my_rows, columns_of(chip)]
    shares = [
        remote(mine, mine, share_send.at[step], share_recv.at[step], peer)
        for step, peer in enumerate(peers)
    ]
    for copy in shares:
        copy.start()
    for copy in shares:
        copy.wait_recv()
    over = remote(
        chosen.at[0, my_rows], chosen.at[1, my_rows], pair_send.at[2], pair_recv.at[2], across
    )
    over.start()
    here = remote(
        chosen.at[0, my_rows], chosen.at[0, my_rows], pair_send.at[3], pair_recv.at[3], twin
    )
    here.start()

    def event(hop, piece):
        @pl.when((hop < half) | (piece == 0))
        def _():
            right(hop, piece).wait_recv()

            @pl.when((hop + 1 < half) | ((hop + 1 == half) & (piece == 0)))
            def _():
                right(hop + 1, piece).start()

            to_twin(2 * hop - 1, piece).start()

        @pl.when((hop < half) | (piece == 1))
        def _():
            left(hop, piece).wait_recv()

            @pl.when((hop + 1 < half) | ((hop + 1 == half) & (piece == 1)))
            def _():
                left(hop + 1, piece).start()

            to_twin(2 * hop - hop // half, piece).start()

    event(1, 0)
    event(1, 1)
    over.wait_recv()
    there = remote(
        chosen.at[1, my_rows], chosen.at[1, my_rows], pair_send.at[4], pair_recv.at[4], twin
    )
    there.start()
    here.wait_recv()
    event(2, 0)
    there.wait_recv()
    for which in range(2):
        own[which * padded : (which + 1) * padded] = jnp.dot(
            choose, chosen[which], preferred_element_type=jnp.float32
        ).astype(own.dtype)
    whiten(own, white_source)

    def cross_block(block, cross):
        for slot in range(slots):
            cross_real = cross_imag = None
            for which in range(2):
                rows = pl.ds(which * receivers, receivers)
                recv_real = everyone[block, rows, :NF]
                recv_imag = everyone[block, rows, NF:]
                at = which * padded + slot
                source_real = white_source[at : at + 1, :NF]
                source_imag = white_source[at : at + 1, NF:]
                term_real = source_real * recv_real + source_imag * recv_imag
                term_imag = source_imag * recv_real - source_real * recv_imag
                cross_real = term_real if cross_real is None else cross_real + term_real
                cross_imag = term_imag if cross_imag is None else cross_imag + term_imag
            cross[slot * receivers : (slot + 1) * receivers, :NF] = cross_real
            cross[slot * receivers : (slot + 1) * receivers, NF:] = cross_imag

    def finish_block(block, cross, index):
        stacked = jnp.dot(cross[...], back_ref[...], preferred_element_type=jnp.float32)
        mean_sq = jnp.mean(stacked * stacked, axis=-1, keepdims=True)
        normed = (stacked * lax.rsqrt(mean_sq + 1e-06)).astype(finished.dtype)
        for slot in range(slots):
            finished[block, slot] = normed[slot * receivers : (slot + 1) * receivers]
        write(block, index).start()

    def write(block, index):
        return pltpu.make_async_copy(finished.at[block], out_hbm.at[:, block], out_sem.at[index])

    def block_of(number, stream):
        return chip_at(place + offset_of(number)) * 2 + stream

    ahead = 3

    @pl.loop(0, chips)
    def _(number):
        now = number + ahead

        @pl.when(now < 2 * half)
        def _():
            event(now // 2 + 1, now % 2)

        for piece in range(2):
            to_twin(number, piece).wait_recv()
        cross_block(block_of(number, 0), cross_even)
        finish_block(block_of(number, 0), cross_even, number * 2)
        cross_block(block_of(number, 1), cross_odd)
        finish_block(block_of(number, 1), cross_odd, number * 2 + 1)

    for copy in deals + shares + [swap, fold, over, here, there]:
        copy.wait_send()

    @pl.loop(0, 2 * half)
    def _(now):
        hop, piece = now // 2 + 1, now % 2

        @pl.when((hop < half) | (piece == 0))
        def _():
            right(hop, piece).wait_send()

        @pl.when((hop < half) | (piece == 1))
        def _():
            left(hop, piece).wait_send()

    @pl.loop(0, chips)
    def _(number):
        for piece in range(2):
            to_twin(number, piece).wait_send()
            write(block_of(number, piece), number * 2 + piece).wait()


def paired(forward, back, traces, live_mask, sources, owners):
    row_count = lax.axis_size("row")
    chips = row_count // 2
    channels, width = traces.shape[1:]
    receivers = channels // 2
    num_sources = sources.shape[0]
    slots = 3 * num_sources // row_count
    padded = -(-slots // 16) * 16
    kind = traces.dtype
    anywhere = pl.BlockSpec(memory_space=pl.ANY)
    dma = pltpu.SemaphoreType.DMA
    hops = chips // 2 * 2
    return pl.pallas_call(
        partial(fused_kernel, chips, slots),
        in_specs=[anywhere] * 6,
        out_specs=anywhere,
        out_shape=jax.ShapeDtypeStruct((slots, row_count, receivers, LAGS), jnp.bfloat16),
        scratch_shapes=[
            pltpu.VMEM((channels, width), kind),
            pltpu.VMEM((1, channels), jnp.int32),
            pltpu.VMEM((1, num_sources), jnp.int32),
            pltpu.VMEM((1, num_sources), jnp.int32),
            pltpu.VMEM(back.shape, kind),
            dma((5,)),
            pltpu.VMEM(forward.shape, kind),
            pltpu.VMEM((channels, width), kind),
            pltpu.VMEM((receivers, width), kind),
            pltpu.VMEM((num_sources, width), kind),
            pltpu.VMEM((num_sources // 2, width), kind),
            pltpu.VMEM((num_sources // 2, width), kind),
            pltpu.VMEM((chips - 1, num_sources // 2, width // chips), kind),
            pltpu.VMEM((2, num_sources, width), kind),
            pltpu.VMEM((2 * padded, 2 * NF), kind),
            pltpu.VMEM((row_count, channels, 2 * NF), kind),
            pltpu.VMEM((slots * receivers, 2 * NF), kind),
            pltpu.VMEM((slots * receivers, 2 * NF), kind),
            pltpu.VMEM((channels, width), kind),
            pltpu.VMEM((2 * padded, width), kind),
            pltpu.VMEM((row_count, slots, receivers, LAGS), kind),
            dma,
            dma((row_count,)),
            dma((5,)), dma((5,)),
            dma((chips - 1,)), dma((chips - 1,)),
            dma((chips - 1,)), dma((chips - 1,)),
            dma((hops,)), dma((hops,)),
            dma((hops,)), dma((hops,)),
            dma((2 * chips,)), dma((2 * chips,)),
        ],
        compiler_params=pltpu.CompilerParams(
            collective_id=0, has_side_effects=True, vmem_limit_bytes=56 << 20
        ),
        cost_estimate=pl.CostEstimate(
            flops=2 * slots * row_count * receivers * 2 * NF * LAGS,
            bytes_accessed=2 * width * 2 * NF,
            transcendentals=0,
        ),
    )(traces[0], live_mask[None, :], sources[None, :], owners.reshape(1, num_sources), forward, back)


def solution(mesh):
    placed = (P(("run", "seg"), "row", "col"), P(("run", "row")), P(), P())
    body = local
    if mesh.shape["col"] == 1 and mesh.shape["seg"] == 2 and mesh.shape["row"] % 4 == 0:
        forward, back = host_tables(NT)
        body = partial(paired, forward, back)
    return jax.shard_map(
        body,
        mesh=mesh,
        in_specs=placed,
        out_specs=P(("run", "row"), None, ("col", "seg"), None),
        check_vma=False,
    )
```

```python
import math
from functools import partial

import jax
import jax.numpy as jnp
import numpy as np
from jax import lax
from jax.experimental import pallas as pl
from jax.experimental.pallas import tpu as pltpu
from jax.sharding import PartitionSpec as P

NT = 2048
NF = 1024
LAGS = 256
BAND = 64


two_pi = 2.0 * math.pi


def turn_table(first_ids, second_ids, period):
    product = first_ids[:, None] * second_ids[None, :] % period
    return product.astype(jnp.float32) * (two_pi / period)


def lag_matrix(bin_ids):
    lag_ids = jnp.arange(LAGS, dtype=jnp.int32) - LAGS // 2 + NT
    lag_angles = turn_table(bin_ids, lag_ids, NT)
    return jnp.concatenate(
        [jnp.cos(lag_angles).astype(jnp.bfloat16), -jnp.sin(lag_angles).astype(jnp.bfloat16)],
        axis=0,
    )


def correlate(recv_real, recv_imag, real_source, imag_source, lag_table):
    cross_real = (
        real_source[:, None, :] * recv_real[:, :, None]
        + imag_source[:, None, :] * recv_imag[:, :, None]
    ).astype(jnp.bfloat16)
    cross_imag = (
        imag_source[:, None, :] * recv_real[:, :, None]
        - real_source[:, None, :] * recv_imag[:, :, None]
    ).astype(jnp.bfloat16)
    stacked_cross = jnp.concatenate([cross_real, cross_imag], axis=0)
    return jnp.einsum("fl,fgv->gvl", lag_table, stacked_cross, preferred_element_type=jnp.float32)


def local(traces, live_mask, sources, owners):
    col_count = lax.axis_size("col")
    seg_count = lax.axis_size("seg")
    row_count = lax.axis_size("row")
    samples = traces[0]
    channels = samples.shape[0]
    local_width = samples.shape[1]
    num_sources = sources.shape[0]
    first_sample = lax.axis_index("col") * local_width
    half_bins = NF // col_count
    sample_ids = first_sample + jnp.arange(local_width, dtype=jnp.int32)
    bin_ids = jnp.arange(half_bins * lax.axis_size("col"), dtype=jnp.int32)
    angles = turn_table(sample_ids, bin_ids, NT)
    cosine = jnp.cos(angles).astype(jnp.bfloat16)
    sine_table = jnp.sin(angles).astype(jnp.bfloat16)
    real_part = jnp.einsum("tf,ct->fc", cosine, samples, preferred_element_type=jnp.float32)
    imag_part = -jnp.einsum("tf,ct->fc", sine_table, samples, preferred_element_type=jnp.float32)
    spectra = lax.psum_scatter(
        jnp.concatenate([real_part, imag_part], axis=1).astype(jnp.bfloat16),
        "col",
        scatter_dimension=0,
        tiled=True,
    ).astype(jnp.float32)
    squares = (spectra * spectra).reshape(half_bins // BAND, BAND, 2, channels)
    band_power = jnp.sum(squares, axis=(1, 2)) / (2 * BAND) + 1e-05
    scaling = live_mask.astype(jnp.float32)[None, :] / jnp.sqrt(band_power)
    scaling = jnp.repeat(scaling, BAND, axis=0)
    whitened = (
        (spectra.reshape(half_bins, 2, channels) * scaling[:, None, :])
        .reshape(half_bins, 2 * channels)
        .astype(jnp.bfloat16)
    )
    white_real = whitened[:, :channels]
    white_imag = whitened[:, channels:]
    everyone = lax.all_gather(whitened, "row", axis=1, tiled=True)
    block_ids = sources // channels
    within = sources % channels
    real_cols = block_ids * (2 * channels) + within
    source_real = jnp.take(everyone, real_cols, axis=1)
    source_imag = jnp.take(everyone, real_cols + channels, axis=1)
    receivers = channels // (col_count * seg_count)
    bin_ids = lax.axis_index("col") * half_bins + jnp.arange(half_bins, dtype=jnp.int32)
    lag_table = lag_matrix(bin_ids)
    real_source = source_real.astype(jnp.float32)
    imag_source = source_imag.astype(jnp.float32)

    def one_group(offset):
        recv_real = lax.dynamic_slice_in_dim(white_real, offset, receivers, 1).astype(jnp.float32)
        recv_imag = lax.dynamic_slice_in_dim(white_imag, offset, receivers, 1).astype(jnp.float32)
        return correlate(recv_real, recv_imag, real_source, imag_source, lag_table)

    offsets = (
        jnp.arange(receivers * lax.axis_size(("col", "seg")) // receivers, dtype=jnp.int32)
        * receivers
    )
    blocks = lax.map(one_group, offsets)
    stacked = lax.psum_scatter(
        blocks.reshape(receivers * lax.axis_size(("col", "seg")), num_sources, LAGS).astype(
            jnp.bfloat16
        ),
        ("col", "seg"),
        scatter_dimension=0,
        tiled=True,
    ).astype(jnp.float32)
    mean_sq = jnp.mean(stacked * stacked, axis=-1, keepdims=True)
    normed = (stacked / jnp.sqrt(mean_sq + 1e-06)).astype(jnp.bfloat16)
    capacity = 3 * num_sources // row_count
    owner_ids = owners[:, 0]
    order_ids = jnp.arange(num_sources, dtype=jnp.int32)
    earlier = (owner_ids[:, None] == owner_ids[None, :]) & (order_ids[None, :] < order_ids[:, None])
    slot_rank = jnp.sum(earlier.astype(jnp.int32), axis=1)
    slot_ids = owner_ids * capacity + slot_rank
    placing = (
        jnp.arange(row_count * capacity, dtype=jnp.int32)[:, None] == slot_ids[None, :]
    ).astype(jnp.bfloat16)
    outgoing = jnp.einsum(
        "sv,gvl->sgl", placing, normed, preferred_element_type=jnp.float32
    ).astype(jnp.bfloat16)
    return lax.all_to_all(outgoing[:, None], "row", split_axis=0, concat_axis=1, tiled=True)


def host_tables(num_samples):
    samples = np.arange(num_samples, dtype=np.int64)
    bins = np.arange(NF, dtype=np.int64)
    angles = (samples[:, None] * bins[None, :] % NT) * (two_pi / NT)
    forward = np.concatenate([np.cos(angles), -np.sin(angles)], axis=1)
    lags = np.arange(LAGS, dtype=np.int64) - LAGS // 2 + NT
    lag_angles = (bins[:, None] * lags[None, :] % NT) * (two_pi / NT)
    back = np.concatenate([np.cos(lag_angles), -np.sin(lag_angles)], axis=0)
    return forward.astype(jnp.bfloat16), back.astype(jnp.bfloat16)


def at_ring(place, lines):
    second = place // lines
    return second, (1 - second) * place + second * (2 * lines - 1 - place)


def fused_kernel(
    chips, slots, traces_hbm, live_hbm, sources_hbm, owners_hbm, forward_hbm, back_hbm, out_hbm,
    traces_ref, live_ref, sources_ref, owners_ref, back_ref, in_sem, forward, samples, given_in, picked, core_in, part, parts_in, chosen, white_source, everyone,
    cross_even, cross_odd, joined, own, finished, table_sem, out_sem, pair_send, pair_recv, deal_send, deal_recv, share_send, share_recv,
    right_send, right_recv, left_send, left_recv, twin_send, twin_recv,
):
    lines = chips // 2
    half = chips // 2
    row = lax.axis_index("row")
    seg = lax.axis_index("seg")
    chip, core = row // 2, row % 2
    line, side = chip // 2, chip % 2
    place = (1 - side) * line + side * (2 * lines - 1 - line)
    channels, width = traces_ref.shape
    receivers = channels // 2
    num_sources = sources_ref.shape[1]
    own_sources = num_sources // 2
    padded = white_source.shape[0] // 2
    columns = width // chips

    def chip_at(where):
        second, first = at_ring((where + chips) % chips, lines)
        return first * 2 + second

    def remote(source, target, send_sem, recv_sem, peer):
        return pltpu.make_async_remote_copy(
            src_ref=source, dst_ref=target, send_sem=send_sem, recv_sem=recv_sem,
            device_id=peer, device_id_type=pl.DeviceIdType.MESH,
        )

    inputs = [
        pltpu.make_async_copy(source, target, in_sem.at[index])
        for index, (source, target) in enumerate((
            (sources_hbm, sources_ref), (owners_hbm, owners_ref), (live_hbm, live_ref),
            (traces_hbm, traces_ref), (back_hbm, back_ref),
        ))
    ]
    for copy in inputs:
        copy.start()
    table_copy = pltpu.make_async_copy(forward_hbm, forward, table_sem)
    table_copy.start()
    twin = {"row": chip * 2 + 1 - core}
    across = {"seg": 1 - seg}
    peers = [{"row": (chip + step) % chips * 2 + core} for step in range(1, chips)]
    barrier = pltpu.get_barrier_semaphore()
    for peer in [twin, across] + peers:
        pl.semaphore_signal(barrier, inc=1, device_id=peer, device_id_type=pl.DeviceIdType.MESH)

    for copy in inputs:
        copy.wait()

    def ids(shape, axis):
        return lax.broadcasted_iota(jnp.int32, shape, axis).astype(jnp.float32)

    def column(values):
        square = (values.shape[1], values.shape[1])
        kept_ones = jnp.where(ids(square, 0) == ids(square, 1), values, 0.0)
        return jnp.sum(kept_ones, axis=1, keepdims=True)

    live = live_ref[...].astype(jnp.float32)
    source_row = sources_ref[...].astype(jnp.float32)
    owner_row = owners_ref[...].astype(jnp.float32)
    my_row = row.astype(jnp.float32)
    samples[...] = traces_ref[...] * column(live).astype(traces_ref.dtype)
    local_ids = ids((num_sources, channels), 1) + my_row * channels
    picking = jnp.where(column(source_row) == local_ids, 1.0, 0.0).astype(samples.dtype)
    picked[...] = jnp.dot(
        picking, samples[...], preferred_element_type=jnp.float32
    ).astype(picked.dtype)
    square = (num_sources, num_sources)
    earlier = jnp.where(ids(square, 0) < ids(square, 1), 1.0, 0.0)
    alike = jnp.where(column(owner_row) == owner_row, earlier, 0.0)
    rank = jnp.sum(alike, axis=0, keepdims=True)
    slot_of = jnp.where(owner_row == my_row, rank, float(padded))
    choose = jnp.where(ids((padded, num_sources), 0) == slot_of, 1.0, 0.0).astype(samples.dtype)
    pl.semaphore_wait(barrier, chips + 1)

    def rows_of(first, count):
        return pl.ds(pl.multiple_of(first, count), count)

    my_rows = rows_of(core * own_sources, own_sources)
    twin_rows = rows_of((1 - core) * own_sources, own_sources)
    swap = remote(
        samples.at[rows_of((1 - seg) * receivers, receivers)], given_in,
        pair_send.at[0], pair_recv.at[0], across,
    )
    fold = remote(picked.at[twin_rows], core_in, pair_send.at[1], pair_recv.at[1], twin)
    fold.start()
    swap.start()

    def columns_of(which):
        return pl.ds(pl.multiple_of(which * columns, columns), columns)

    fold.wait_recv()
    part[...] = picked[my_rows, :] + core_in[...]
    deals = []
    for step, peer in enumerate(peers):
        deals.append(remote(
            part.at[:, columns_of((chip + step + 1) % chips)], parts_in.at[step],
            deal_send.at[step], deal_recv.at[step], peer,
        ))
    for copy in deals:
        copy.start()

    chunk = 4 * BAND

    def whiten(traces, target):
        first = lax.broadcasted_iota(jnp.int32, (chunk, chunk), 0) // BAND
        second = lax.broadcasted_iota(jnp.int32, (chunk, chunk), 1) // BAND
        same = jnp.where(first == second, 1.0, 0.0).astype(jnp.bfloat16)

        @pl.loop(0, NF // chunk)
        def _(step):
            low = pl.ds(pl.multiple_of(step * chunk, chunk), chunk)
            high = pl.ds(pl.multiple_of(NF + step * chunk, chunk), chunk)
            real = jnp.dot(traces[...], forward[:, low], preferred_element_type=jnp.float32)
            imag = jnp.dot(traces[...], forward[:, high], preferred_element_type=jnp.float32)
            power = real * real + imag * imag
            upper = power.astype(jnp.bfloat16)
            lower = (power - upper.astype(jnp.float32)).astype(jnp.bfloat16)
            total = jnp.dot(upper, same, preferred_element_type=jnp.float32) + jnp.dot(
                lower, same, preferred_element_type=jnp.float32
            )
            scaling = lax.rsqrt(total / (2 * BAND) + 1e-05)
            target[:, low] = (real * scaling).astype(jnp.bfloat16)
            target[:, high] = (imag * scaling).astype(jnp.bfloat16)

    for copy in deals:
        copy.wait_recv()
    total = part[:, columns_of(chip)].astype(jnp.float32)
    for step in range(chips - 1):
        total = total + parts_in[step].astype(jnp.float32)
    chosen[0, my_rows, columns_of(chip)] = total.astype(chosen.dtype)
    mine = chosen.at[0, my_rows, columns_of(chip)]
    shares = [
        remote(mine, mine, share_send.at[step], share_recv.at[step], peer)
        for step, peer in enumerate(peers)
    ]
    for copy in shares:
        copy.start()
    table_copy.wait()
    swap.wait_recv()
    joined[:receivers] = samples[rows_of(seg * receivers, receivers), :]
    joined[receivers:] = given_in[...]
    whiten(joined, everyone.at[row])

    def shard(where, stream, piece):
        return everyone.at[chip_at(where) * 2 + stream, pl.ds(piece * receivers, receivers)]

    right_peer = {"row": chip_at(place + 1) * 2 + core}
    left_peer = {"row": chip_at(place - 1) * 2 + core}

    def right(hop, piece):
        index = (hop - 1) * 2 + piece
        block = shard(place - hop + 1, core, piece)
        return remote(block, block, right_send.at[index], right_recv.at[index], right_peer)

    def left(hop, piece):
        index = (hop - 1) * 2 + piece
        block = shard(place + hop - 1, core, piece)
        return remote(block, block, left_send.at[index], left_recv.at[index], left_peer)

    def offset_of(number):
        return (number + 1) // 2 * (1 - 2 * (number % 2))

    def to_twin(number, piece):
        index = number * 2 + piece
        block = shard(place + offset_of(number), core, piece)
        return remote(block, block, twin_send.at[index], twin_recv.at[index], twin)

    for piece in range(2):
        right(1, piece).start()
        left(1, piece).start()
    for piece in range(2):
        to_twin(0, piece).start()

    for copy in shares:
        copy.wait_recv()
    over = remote(
        chosen.at[0, my_rows], chosen.at[1, my_rows], pair_send.at[2], pair_recv.at[2], across
    )
    over.start()
    here = remote(
        chosen.at[0, my_rows], chosen.at[0, my_rows], pair_send.at[3], pair_recv.at[3], twin
    )
    here.start()

    def event(hop, piece):
        @pl.when((hop < half) | (piece == 0))
        def _():
            right(hop, piece).wait_recv()

            @pl.when((hop + 1 < half) | ((hop + 1 == half) & (piece == 0)))
            def _():
                right(hop + 1, piece).start()

            to_twin(2 * hop - 1, piece).start()

        @pl.when((hop < half) | (piece == 1))
        def _():
            left(hop, piece).wait_recv()

            @pl.when((hop + 1 < half) | ((hop + 1 == half) & (piece == 1)))
            def _():
                left(hop + 1, piece).start()

            to_twin(2 * hop - hop // half, piece).start()

    event(1, 0)
    event(1, 1)
    over.wait_recv()
    there = remote(
        chosen.at[1, my_rows], chosen.at[1, my_rows], pair_send.at[4], pair_recv.at[4], twin
    )
    there.start()
    here.wait_recv()
    event(2, 0)
    there.wait_recv()
    for which in range(2):
        own[which * padded : (which + 1) * padded] = jnp.dot(
            choose, chosen[which], preferred_element_type=jnp.float32
        ).astype(own.dtype)
    whiten(own, white_source)

    def cross_block(block, cross):
        for slot in range(slots):
            cross_real = cross_imag = None
            for which in range(2):
                rows = pl.ds(which * receivers, receivers)
                recv_real = everyone[block, rows, :NF]
                recv_imag = everyone[block, rows, NF:]
                at = which * padded + slot
                source_real = white_source[at : at + 1, :NF]
                source_imag = white_source[at : at + 1, NF:]
                term_real = source_real * recv_real + source_imag * recv_imag
                term_imag = source_imag * recv_real - source_real * recv_imag
                cross_real = term_real if cross_real is None else cross_real + term_real
                cross_imag = term_imag if cross_imag is None else cross_imag + term_imag
            cross[slot * receivers : (slot + 1) * receivers, :NF] = cross_real
            cross[slot * receivers : (slot + 1) * receivers, NF:] = cross_imag

    def finish_block(block, cross, index):
        stacked = jnp.dot(cross[...], back_ref[...], preferred_element_type=jnp.float32)
        mean_sq = jnp.mean(stacked * stacked, axis=-1, keepdims=True)
        normed = (stacked * lax.rsqrt(mean_sq + 1e-06)).astype(finished.dtype)
        for slot in range(slots):
            finished[block, slot] = normed[slot * receivers : (slot + 1) * receivers]
        write(block, index).start()

    def write(block, index):
        return pltpu.make_async_copy(finished.at[block], out_hbm.at[:, block], out_sem.at[index])

    def block_of(number, stream):
        return chip_at(place + offset_of(number)) * 2 + stream

    ahead = 3

    @pl.loop(0, chips)
    def _(number):
        now = number + ahead

        @pl.when(now < 2 * half)
        def _():
            event(now // 2 + 1, now % 2)

        for piece in range(2):
            to_twin(number, piece).wait_recv()
        cross_block(block_of(number, 0), cross_even)
        finish_block(block_of(number, 0), cross_even, number * 2)
        cross_block(block_of(number, 1), cross_odd)
        finish_block(block_of(number, 1), cross_odd, number * 2 + 1)

    for copy in deals + shares + [swap, fold, over, here, there]:
        copy.wait_send()

    @pl.loop(0, 2 * half)
    def _(now):
        hop, piece = now // 2 + 1, now % 2

        @pl.when((hop < half) | (piece == 0))
        def _():
            right(hop, piece).wait_send()

        @pl.when((hop < half) | (piece == 1))
        def _():
            left(hop, piece).wait_send()

    @pl.loop(0, chips)
    def _(number):
        for piece in range(2):
            to_twin(number, piece).wait_send()
            write(block_of(number, piece), number * 2 + piece).wait()


def paired(forward, back, traces, live_mask, sources, owners):
    row_count = lax.axis_size("row")
    chips = row_count // 2
    channels, width = traces.shape[1:]
    receivers = channels // 2
    num_sources = sources.shape[0]
    slots = 3 * num_sources // row_count
    padded = -(-slots // 16) * 16
    kind = traces.dtype
    anywhere = pl.BlockSpec(memory_space=pl.ANY)
    dma = pltpu.SemaphoreType.DMA
    hops = chips // 2 * 2
    return pl.pallas_call(
        partial(fused_kernel, chips, slots),
        in_specs=[anywhere] * 6,
        out_specs=anywhere,
        out_shape=jax.ShapeDtypeStruct((slots, row_count, receivers, LAGS), jnp.bfloat16),
        scratch_shapes=[
            pltpu.VMEM((channels, width), kind),
            pltpu.VMEM((1, channels), jnp.int32),
            pltpu.VMEM((1, num_sources), jnp.int32),
            pltpu.VMEM((1, num_sources), jnp.int32),
            pltpu.VMEM(back.shape, kind),
            dma((5,)),
            pltpu.VMEM(forward.shape, kind),
            pltpu.VMEM((channels, width), kind),
            pltpu.VMEM((receivers, width), kind),
            pltpu.VMEM((num_sources, width), kind),
            pltpu.VMEM((num_sources // 2, width), kind),
            pltpu.VMEM((num_sources // 2, width), kind),
            pltpu.VMEM((chips - 1, num_sources // 2, width // chips), kind),
            pltpu.VMEM((2, num_sources, width), kind),
            pltpu.VMEM((2 * padded, 2 * NF), kind),
            pltpu.VMEM((row_count, channels, 2 * NF), kind),
            pltpu.VMEM((slots * receivers, 2 * NF), kind),
            pltpu.VMEM((slots * receivers, 2 * NF), kind),
            pltpu.VMEM((channels, width), kind),
            pltpu.VMEM((2 * padded, width), kind),
            pltpu.VMEM((row_count, slots, receivers, LAGS), kind),
            dma,
            dma((row_count,)),
            dma((5,)), dma((5,)),
            dma((chips - 1,)), dma((chips - 1,)),
            dma((chips - 1,)), dma((chips - 1,)),
            dma((hops,)), dma((hops,)),
            dma((hops,)), dma((hops,)),
            dma((2 * chips,)), dma((2 * chips,)),
        ],
        compiler_params=pltpu.CompilerParams(
            collective_id=0, has_side_effects=True, vmem_limit_bytes=56 << 20
        ),
        cost_estimate=pl.CostEstimate(
            flops=2 * slots * row_count * receivers * 2 * NF * LAGS,
            bytes_accessed=2 * width * 2 * NF,
            transcendentals=0,
        ),
    )(traces[0], live_mask[None, :], sources[None, :], owners.reshape(1, num_sources), forward, back)


def solution(mesh):
    placed = (P(("run", "seg"), "row", "col"), P(("run", "row")), P(), P())
    body = local
    if mesh.shape["col"] == 1 and mesh.shape["seg"] == 2 and mesh.shape["row"] % 4 == 0:
        forward, back = host_tables(NT)
        body = partial(paired, forward, back)
    return jax.shard_map(
        body,
        mesh=mesh,
        in_specs=placed,
        out_specs=P(("run", "row"), None, ("col", "seg"), None),
        check_vma=False,
    )
```
